32 devices in a mesh: xs: 8 (over z, y), ys: 4 (over x, core).
Axes of the slice: x: 2, y: 2, z: 4, core: 2. Of those that a mesh axis runs over, the one named last changes fastest.
Arguments:
- multipoles: bfloat16 [121, 4096], P(None, ('xs', 'ys')), may hold values from -6 to 6
- translation_ops: bfloat16 [316, 121, 121], replicated, may hold values from -0.046875 to 0.046875
- target_interaction_table: int32 [316, 4096], P(None, ('xs', 'ys')), may hold values from -1 to 1151, as said below
- evaluation: bfloat16 [4, 121, 65536], P(None, None, ('xs', 'ys')), may hold values from -0.5 to 0.5
- ion_data: bfloat16 [4, 65536], P(None, ('xs', 'ys')), may hold values from -1 to 1
- atom_owner: int32 [65536, 1], P(('xs', 'ys')), may hold values from 0 to 31, as said below
- atom_slot: int32 [65536], P(('xs', 'ys')), may hold values from 0 to 127
Outputs:
- local_exp: bfloat16 [121, 4096], P(None, ('xs', 'ys'))
- atom_far_field: float32 [4, 65536], P(None, ('xs', 'ys'))
- box_virial: float32 [9, 4096], P(None, ('xs', 'ys'))
The draws below stay inside these ranges and needn't reach their ends.
Inputs may be any that keep to these rules, and one draw needn't show every extreme that they name: `target_interaction_table`: box slot s of a device is (bx * 4 + by) * 8 + bz; device (ix, iy) holds the periodic grid's boxes of x from ix * 4, y from iy * 4 and all z. Row k stands for the k-th offset (dx, dy, dz) of -3..3 in each coordinate, dx slowest, dz fastest, leaving out those with all three of magnitude 1 or less. An entry is -1, or (3 * (ex + 1) + (ey + 1)) * 128 + s naming the box at that offset from the target: slot s of the device ex steps along xs and ey steps along ys away, ex and ey in -1, 0, 1. It is -1 where the offset along some coordinate lies outside -2 - q .. 3 - q, q the parity of the target's coordinate there, and where the box at that offset holds no ions; most boxes hold ions. `atom_owner`: the device is ix * 4 + iy; an atom held by device (ix, iy) names that device itself or one of the eight devices ((ix + ex) mod 8, (iy + ey) mod 4) with ex, ey in -1, 0, 1; among the atoms of one device at most 32 name the same other device, and in every device's atoms some other device is named exactly 32 times.
All inputs are finite; a program needn't handle non-finite values.
Results may differ from the reference program's by a relative error of at most 0.0029.
Values may be sent and summed in bfloat16 or wider, within the bound.
No kernel may reach another device: no remote copies, remote signals or barrier semaphores. Data moves between devices by JAX's collectives and lax.ppermute only.
A program may use at most 64 MiB of HBM per device.

```python
import jax
import jax.numpy as jnp
import numpy as np
from jax import lax

P_SIZE = 121
NOFF = 316
BXD = 4
BYD = 4
BZ = 8
ATOMS_DEV = 2048
CAP = 128
NBOX = 4096
ATOMS = 65536
SEND = 32
GX = 32
GY = 16
N_XS = 8
N_YS = 4
DEVICES = 32


def offset_table():
    listed = []
    for shift_x in range(-3, 4):
        for shift_y in range(-3, 4):
            for shift_z in range(-3, 4):
                if max(abs(shift_x), abs(shift_y), abs(shift_z)) >= 2:
                    listed.append((shift_x, shift_y, shift_z))
    return np.array(listed, dtype=np.int32)


def inside_list(coord, delta):
    parity = coord % 2
    return (delta >= -2 - parity) & (delta <= 3 - parity)


def draw_target_interaction_table(key, part):
    table = jnp.asarray(offset_table())
    filled = jax.random.randint(jax.random.fold_in(key, 7), (GX, GY, BZ), 0, 10) < 7
    targets = jnp.arange(NBOX, dtype=jnp.int32)
    device = targets // CAP
    home_x = (device // N_YS)[None, :]
    home_y = (device % N_YS)[None, :]
    slot = targets % CAP
    box_x = (slot // (BYD * BZ))[None, :]
    box_y = (slot // BZ % BYD)[None, :]
    box_z = (slot % BZ)[None, :]
    delta_x = table[:, 0:1]
    delta_y = table[:, 1:2]
    delta_z = table[:, 2:3]
    valid = inside_list(box_x, delta_x) & inside_list(box_y, delta_y) & inside_list(box_z, delta_z)
    reach_x = box_x + delta_x
    reach_y = box_y + delta_y
    step_x = jnp.floor_divide(reach_x, BXD)
    stride_along_y = jnp.floor_divide(reach_y, BYD)
    source_x = reach_x - step_x * BXD
    source_y = reach_y - stride_along_y * BYD
    source_z = jnp.remainder(box_z + delta_z, BZ)
    global_x = jnp.remainder(home_x * BXD + reach_x, GX)
    global_y = jnp.remainder(home_y * BYD + reach_y, GY)
    held = filled[global_x, global_y, source_z]
    entry = (3 * (step_x + 1) + (stride_along_y + 1)) * CAP + (source_x * BYD + source_y) * BZ + source_z
    return jnp.where(valid & held, entry, -1).astype(jnp.int32)


def neighbour_shifts():
    listed = []
    for shift_x in (-1, 0, 1):
        for shift_y in (-1, 0, 1):
            if shift_x != 0 or shift_y != 0:
                listed.append((shift_x, shift_y))
    return np.array(listed, dtype=np.int32)


def draw_atom_owner(key, part):
    shifts = jnp.asarray(neighbour_shifts())

    def one_device(device):
        own_key = jax.random.fold_in(key, device)
        counts = jax.random.randint(jax.random.fold_in(own_key, 1), (8,), SEND // 2, SEND + 1)
        fullest = jax.random.randint(jax.random.fold_in(own_key, 2), (), 0, 8)
        counts = jnp.where(jnp.arange(8, dtype=jnp.int32) == fullest, SEND, counts).astype(jnp.int32)
        ends = jnp.cumsum(counts)
        position = jnp.arange(ATOMS_DEV, dtype=jnp.int32)
        which = jnp.sum((position[:, None] >= ends[None, :]).astype(jnp.int32), axis=1)
        home_x = device // N_YS
        home_y = device % N_YS
        nearby = (home_x + shifts[:, 0]) % N_XS * N_YS + (home_y + shifts[:, 1]) % N_YS
        choices_all = jnp.concatenate([nearby, jnp.reshape(device, (1,))]).astype(jnp.int32)
        owners = choices_all[which]
        order = jax.random.permutation(jax.random.fold_in(own_key, 3), ATOMS_DEV)
        return owners[order]
    owners = jax.vmap(one_device)(jnp.arange(DEVICES, dtype=jnp.int32))
    return owners.reshape(ATOMS, 1).astype(jnp.int32)


def place_ends(result, key, smallest, high):
    longest = result.shape.index(max(result.shape))
    spots = []
    for shift in (0, 1):
        where = [jax.random.randint(jax.random.fold_in(key, axis), (), 0, length) for axis, length in enumerate(result.shape)]
        where[longest] = (where[longest] + shift) % result.shape[longest]
        spots.append(tuple(where))
    return result.at[spots[0]].set(smallest).at[spots[1]].set(high)


def shard_levels(key, extent, pieces, least, high):
    def one(axis_at, blocks):
        steps = jax.random.uniform(jax.random.fold_in(jax.random.fold_in(key, 6), axis_at), (blocks,), jnp.float32, least / len(pieces), high / len(pieces))
        return jnp.repeat(jnp.exp(steps), extent[axis_at] // blocks).reshape((-1,) + (1,) * (len(extent) - axis_at - 1))

    loudness = one(*pieces[0])
    for cut in pieces[1:]:
        loudness = loudness * one(*cut)
    return loudness


def scatter_about(key, shape, spread, most, shards=(), kind=jnp.bfloat16):
    values = spread * jax.random.normal(key, shape, jnp.float32)
    if shards:
        values = values * shard_levels(key, shape, shards, -0.22, 0.18)
    return jnp.clip(values, -most, most).astype(kind)


def setup_inputs(seed: int = 0) -> dict:
    streams_of = jax.random.split(jax.random.key(seed), 8)
    return {
        "multipoles": scatter_about(streams_of[0], (P_SIZE, NBOX), 1.0, 6.0, ((1, 32),)),
        "translation_ops": scatter_about(streams_of[1], (NOFF, P_SIZE, P_SIZE), (P_SIZE * 132) ** -0.5, 0.046875),
        "target_interaction_table": draw_target_interaction_table(jax.random.fold_in(streams_of[7], 71), 0),
        "evaluation": scatter_about(streams_of[3], (4, P_SIZE, ATOMS), P_SIZE ** -0.5, 0.5, ((2, 32),)),
        "ion_data": jnp.clip(jax.random.uniform(streams_of[4], (4, ATOMS), jnp.float32, -1.0, 1.0) * shard_levels(streams_of[4], (4, ATOMS), ((1, 32),), -0.4, 0.0), -1.0, 1.0).astype(jnp.bfloat16),
        "atom_owner": draw_atom_owner(jax.random.fold_in(streams_of[7], 71), 0),
        "atom_slot": place_ends(jax.random.randint(streams_of[6], (ATOMS,), 0, CAP), jax.random.fold_in(streams_of[6], 1), 0, CAP - 1).astype(jnp.int32),
    }


def reference(multipoles, translation_ops, target_interaction_table, evaluation, ion_data, atom_owner, atom_slot):
    nbox = multipoles.shape[1]
    targets = jnp.arange(nbox, dtype=jnp.int32)
    device = targets // CAP
    home_x = device // N_YS
    home_y = device % N_YS
    padded = jnp.concatenate([multipoles.astype(jnp.float32), jnp.zeros((P_SIZE, 1), jnp.float32)], axis=1)

    def step(total, item):
        translation_matrix, entries = item
        valid = entries >= 0
        safe = jnp.where(valid, entries, 0).astype(jnp.int32)
        shift_x = safe // (3 * CAP) - 1
        shift_y = (safe // CAP) % 3 - 1
        source_dev = ((home_x + shift_x) % N_XS) * N_YS + (home_y + shift_y) % N_YS
        source_box_index = jnp.where(valid, source_dev * CAP + safe % CAP, nbox).astype(jnp.int32)
        gathered = jnp.take(padded, source_box_index, axis=1)
        return total + jnp.dot(translation_matrix.astype(jnp.float32), gathered), None

    total, _ = lax.scan(step, jnp.zeros((P_SIZE, nbox), jnp.float32), (translation_ops, target_interaction_table))
    local_exp = total.astype(jnp.bfloat16)

    box = (atom_owner[:, 0] * CAP + atom_slot).astype(jnp.int32)
    box_cols = jnp.take(local_exp, box, axis=1).astype(jnp.float32)
    atom_far_field = jnp.stack([jnp.sum(evaluation[c].astype(jnp.float32) * box_cols, axis=0) for c in range(4)])

    charge = ion_data[0].astype(jnp.float32)
    position = ion_data[1:4].astype(jnp.float32)
    virial_terms = (charge[None, None, :] * position[:, None, :] * atom_far_field[None, 1:4, :]).reshape(9, -1)
    box_virial = jax.ops.segment_sum(virial_terms.T, box, num_segments=nbox).T
    return local_exp, atom_far_field, box_virial
```

```python
import functools

import jax
import jax.numpy as jnp
from jax import lax
from jax.experimental import pallas as pl
from jax.experimental.pallas import tpu as pltpu
from jax.sharding import PartitionSpec as P

BF = jnp.bfloat16
F32 = jnp.float32
REACH = 3
NSHIFT = 2 * REACH + 1
LANES = 128
BX = 4
BY = 4
BZ = 8
EXT = BX + 2 * REACH
SLAB_X = REACH * BY * BZ
SLAB_Y = BX * REACH * BZ + 2 * REACH * REACH * BZ
FIELDS = 4
STEP = 40
AROUND = [(1, 1), (1, 0), (1, 2), (2, 1), (2, 0), (2, 2), (0, 1), (0, 2)]
SENDERS = [(0, 1), (1, 1), (2, 1), (0, 2), (1, 2), (2, 2), (1, 0), (2, 0)]


def offsets():
    listed = []
    for dx in range(-REACH, REACH + 1):
        for dy in range(-REACH, REACH + 1):
            for dz in range(-REACH, REACH + 1):
                if max(abs(dx), abs(dy), abs(dz)) >= 2:
                    listed.append((dx, dy, dz))
    return listed


def up(value, unit):
    return -(-value // unit) * unit


def by_operator_kernel(first, ops_ref, out_ref, held, sems):
    terms, noff, _ = ops_ref.shape
    total = out_ref.shape[0]
    part = up(total // 4, 16)
    cuts = [slice(k, min(k + part, noff)) for k in range(0, noff, part)]
    copies = {}
    for j in range(held.shape[0]):
        q = (first + j) * 16
        some = min(16, terms - q)
        for n, cut in enumerate(cuts if j == 0 else [slice(0, noff)]):
            copies[j, cut.start] = pltpu.make_async_copy(
                ops_ref.at[q : q + some, cut, :], held.at[j, :some, cut, :], sems.at[n if j == 0 else j + len(cuts) - 1]
            )
            copies[j, cut.start].start()
    for j in range(held.shape[0]):
        some = min(16, terms - (first + j) * 16)
        rows = slice(16 * j, 16 * j + 16)
        for k0 in range(0, total, 16):
            if (j, k0) in copies:
                copies[j, k0].wait()
            x = held[j, :some, k0 : min(k0 + 16, noff), :]
            if k0 + 16 > noff:
                x = jnp.concatenate([x.astype(F32), jnp.zeros((some, k0 + 16 - noff, terms), F32)], axis=1).astype(BF)
            if some < 16:
                x = jnp.concatenate([x, jnp.zeros((16 - some, 16, terms), BF)], axis=0)
            x = jnp.swapaxes(x, 0, 1)
            x = jnp.concatenate([x, jnp.zeros((16, 16, LANES - terms), BF)], axis=2)
            out_ref[k0 : k0 + 16, rows, :] = x


def by_operator(ops, first, steps):
    noff, terms, _ = ops.shape
    total = up(noff, 16)
    return pl.pallas_call(
        functools.partial(by_operator_kernel, first),
        in_specs=[pl.BlockSpec(memory_space=pl.ANY)],
        out_specs=pl.BlockSpec(memory_space=pltpu.VMEM),
        out_shape=pltpu.VMEM((total, steps * 16, LANES), BF),
        scratch_shapes=[pltpu.VMEM((steps, 16, noff, terms), BF), pltpu.SemaphoreType.DMA((steps + 3,))],
        compiler_params=pltpu.CompilerParams(vmem_limit_bytes=16 * 2**20),
        cost_estimate=pl.CostEstimate(flops=0, bytes_accessed=2 * total * steps * 16 * LANES * 2, transcendentals=0),
        name="by_operator",
    )(pltpu.with_memory_space_constraint(jnp.transpose(ops, (1, 0, 2)), pltpu.HBM))


INNER = [(3, None), (4, None), (5, None), (2, 1), (6, 0)]
OUTER = [(1, None), (2, None), (6, None), (7, None), (0, 1), (8, 0)]


def shift_sources(pairs, grid, out_ref):
    parity = lax.broadcasted_iota(jnp.int32, (BZ, LANES), 0) % 2
    nothing = jnp.zeros((BZ, LANES), F32)
    for dz in range(-REACH, REACH + 1):
        for x in range(EXT):
            turned = {}

            def tile(y):
                if y not in turned:
                    t = grid[x, y]
                    if dz:
                        t = pltpu.roll(t, (-dz) % BZ, 0)
                    if abs(dz) == REACH:
                        t = jnp.where(parity == (0 if dz > 0 else 1), t, 0.0)
                    turned[y] = t
                return turned[y]

            for n, (y, keep) in enumerate(pairs):
                halves = [tile(y + i) if keep in (None, i) else nothing for i in range(2)]
                out_ref[((dz + REACH) * len(pairs) + n) * EXT + x] = jnp.concatenate(halves, axis=0).astype(BF)


def shifted_sources(inner, outer, offset):
    dx, dy, dz = offset
    tiles = []
    for bx in range(BX):
        for h in range(2):
            pair = (dy + REACH + 2 * h, {-REACH: 1, REACH: 0}.get(dy))
            ref, pairs = (inner, INNER) if pair in INNER else (outer, OUTER)
            if abs(dx) == REACH and bx % 2 != (0 if dx > 0 else 1):
                tiles.append(jnp.zeros((16, LANES), BF))
            else:
                tiles.append(ref[((dz + REACH) * len(pairs) + pairs.index(pair)) * EXT + REACH + dx + bx])
    return jnp.concatenate(tiles, axis=0)


def one_hot(index, rows):
    at = lax.broadcasted_iota(jnp.int32, (rows, index.shape[1]), 0)
    return (at == index).astype(F32).astype(BF)


def split3(x):
    high = x.astype(BF).astype(F32)
    middle = (x - high).astype(BF).astype(F32)
    return jnp.concatenate([high, middle, x - high - middle], axis=0).astype(BF)


def nt(a, b):
    return lax.dot_general(a, b, (((1,), (1,)), ((), ())), preferred_element_type=F32)


def neighbours(size_x, size_y):
    ix, iy = lax.axis_index("xs"), lax.axis_index("ys")
    step_x = [0, 1 - 2 * lax.rem(ix, 2), 2 * lax.rem(ix, 2) - 1]
    step_y = [0, 1 - 2 * lax.rem(iy, 2), 2 * lax.rem(iy, 2) - 1]
    return [
        lax.rem(ix + step_x[x] + size_x, size_x) * size_y + lax.rem(iy + step_y[y] + size_y, size_y)
        for x, y in AROUND
    ]


def pack_kernel(sizes, owner_hbm, slot_hbm, table_hbm, multipoles_hbm, evaluation_ref, ion_hbm,
                own_ref, x_even_ref, x_odd_ref, y_even_ref, y_odd_ref, rows_ref, place_ref,
                held, owner_ref, slot_ref, table_ref, multipoles_ref, ion_ref, sems):
    terms = multipoles_ref.shape[0]
    groups = held.shape[0]
    above = offsets().index((0, 0, 2))
    small = [(table_hbm.at[above // 8 * 8 : above // 8 * 8 + 8, :], table_ref), (multipoles_hbm, multipoles_ref),
             (owner_hbm, owner_ref), (slot_hbm, slot_ref), (ion_hbm, ion_ref)]
    copies = [pltpu.make_async_copy(evaluation_ref.at[:, 16 * j : 16 * j + 16, :], held.at[j], sems.at[j])
              for j in range(groups)]
    copies += [pltpu.make_async_copy(a, b, sems.at[groups + i]) for i, (a, b) in enumerate(small)]
    for copy in copies[groups:] + copies[:groups]:
        copy.start()
    for copy in copies[groups:]:
        copy.wait()
    chunks = slot_ref.shape[0]
    per_peer = place_ref.shape[0] // 8
    row = table_ref[above % 8 : above % 8 + 1, :]
    z = lax.broadcasted_iota(jnp.int32, row.shape, 1) % BZ
    row = jnp.where(z >= 2, pltpu.roll(row, 2, 1), pltpu.roll(row, LANES - 6, 1))
    masked = jnp.where(row >= 0, multipoles_ref[...].astype(F32), 0.0)
    masked = jnp.concatenate([masked, jnp.zeros((LANES - terms, LANES), F32)], axis=0).T
    own_ref[...] = masked.astype(BF)
    even_x = lax.rem(lax.axis_index("xs"), 2) == 0
    lower, upper = masked[:SLAB_X], masked[LANES - SLAB_X :]
    x_even_ref[:SLAB_X] = jnp.where(even_x, upper, lower).astype(BF)
    x_odd_ref[:SLAB_X] = jnp.where(even_x, lower, upper).astype(BF)

    owner = owner_ref[...]
    member = [(owner == device).astype(F32) for device in neighbours(*sizes)]
    stacked = jnp.concatenate(member, axis=0).astype(BF)
    n = 8 * chunks
    r = lax.broadcasted_iota(jnp.int32, (n, n), 0)
    c = lax.broadcasted_iota(jnp.int32, (n, n), 1)
    earlier = ((r // chunks == c // chunks) & (c < r)).astype(F32).astype(BF)
    r = lax.broadcasted_iota(jnp.int32, (LANES, LANES), 0)
    c = lax.broadcasted_iota(jnp.int32, (LANES, LANES), 1)
    before = (r < c).astype(F32).astype(BF)
    ones = jnp.ones((LANES, LANES), BF)
    ahead = jnp.dot(earlier, stacked, preferred_element_type=F32).astype(BF)
    rank = jnp.dot(stacked, before, preferred_element_type=F32) + jnp.dot(ahead, ones, preferred_element_type=F32)
    place = jnp.full((chunks, LANES), -1.0, F32)
    for d in range(8):
        place = jnp.where(member[d] > 0, rank[d * chunks : (d + 1) * chunks] + d * per_peer, place)
    place = place.astype(jnp.int32)
    for j in range(chunks):
        place_ref[:, j * LANES : (j + 1) * LANES] = one_hot(place[j : j + 1], 8 * per_peer)

    half_way = groups // 2 * 4 * LANES

    def picked_by(first, last):
        x = rows_ref[:, :, first:last].reshape(FIELDS * LANES, last - first)
        return nt(x, place_ref[:, first:last])

    slot = slot_ref[...].astype(F32)
    for j in range(chunks // 4):
        part = slice(16 * j, 16 * j + 16)
        if j == groups // 2:
            picked = picked_by(0, half_way)
        slots = [jnp.broadcast_to(slot[4 * j + i : 4 * j + i + 1], (4, LANES)) for i in range(4)]
        extra = [ion_ref[part, :], jnp.concatenate(slots, axis=0).astype(BF)]
        extra = jnp.concatenate([e.reshape(1, 16, LANES) for e in extra], axis=0)
        copies[j].wait()
        for p in range(0, LANES, 16):
            x = held[j, p : min(p + 16, terms)]
            if p + 16 > terms:
                x = jnp.concatenate([x, extra, jnp.zeros((16 - x.shape[0] - 2, 16, LANES), BF)], axis=0)
            x = jnp.swapaxes(x, 0, 1)
            for i in range(4):
                lanes = slice((4 * j + i) * LANES, (4 * j + i + 1) * LANES)
                for f in range(FIELDS):
                    rows_ref[f, p : p + 16, lanes] = x[4 * i + f]

    picked = picked + picked_by(half_way, place_ref.shape[1])

    targets = {
        (1, 1): (x_even_ref, 0), (1, 0): (x_even_ref, 1), (1, 2): (x_even_ref, 2),
        (2, 1): (x_odd_ref, 0), (2, 0): (x_odd_ref, 1), (2, 2): (x_odd_ref, 2),
        (0, 1): (y_even_ref, 0), (0, 2): (y_odd_ref, 0),
    }
    lane = lax.broadcasted_iota(jnp.int32, (LANES, LANES), 1) // per_peer
    each = LANES // per_peer
    turned = []
    for half in range(2):
        x = [picked[f * LANES : (f + 1) * LANES, half * LANES : (half + 1) * LANES] for f in range(FIELDS)]
        turned.append([pltpu.roll(t, f * per_peer, 1) if f else t for f, t in enumerate(x)])
    for d, where in enumerate(AROUND):
        message = turned[d // each][0]
        for f in range(1, FIELDS):
            message = jnp.where(lane == (f + d) % each, turned[d // each][f], message)
        ref, at = targets[where]
        at = at * LANES + (SLAB_X if where[0] else 0)
        ref[at : at + LANES] = message.astype(BF)


def pack(sizes, owner, slot, table, multipoles, evaluation, ions):
    terms = multipoles.shape[0]
    atoms = slot.shape[0]
    chunks = atoms // LANES
    per_peer = atoms // 64
    whole = pl.BlockSpec(memory_space=pltpu.VMEM)
    view = evaluation.transpose(1, 0, 2).reshape(terms, FIELDS, chunks, LANES)
    view = view.transpose(0, 2, 1, 3).reshape(terms, FIELDS * chunks, LANES)
    ions = ions.reshape(FIELDS, chunks, LANES).transpose(1, 0, 2).reshape(FIELDS * chunks, LANES)
    block = lambda rows: jax.ShapeDtypeStruct((rows, LANES), BF)
    return pl.pallas_call(
        functools.partial(pack_kernel, sizes),
        in_specs=[pl.BlockSpec(memory_space=pl.ANY)] * 6,
        out_specs=[whole] * 7,
        out_shape=[block(LANES), block(SLAB_X + 3 * LANES), block(SLAB_X + 3 * LANES), block(LANES), block(LANES),
                   pltpu.VMEM((FIELDS, LANES, atoms), BF),
                   pltpu.VMEM((8 * per_peer, atoms), BF)],
        scratch_shapes=[
            pltpu.VMEM((chunks // 4, terms, 16, LANES), BF),
            pltpu.VMEM((chunks, LANES), jnp.int32),
            pltpu.VMEM((chunks, LANES), jnp.int32),
            pltpu.VMEM((8, LANES), jnp.int32),
            pltpu.VMEM((terms, LANES), BF),
            pltpu.VMEM((FIELDS * chunks, LANES), BF),
            pltpu.SemaphoreType.DMA((chunks // 4 + 5,)),
        ],
        compiler_params=pltpu.CompilerParams(vmem_limit_bytes=24 * 2**20),
        name="pack",
    )(*(pltpu.with_memory_space_constraint(x, pltpu.HBM) for x in (
        owner.reshape(chunks, LANES), slot.reshape(chunks, LANES), table, multipoles, view, ions)))


def tiles_of(ref, first, shape):
    nx, ny = shape
    value = ref[first : first + nx * ny * BZ, :].astype(F32)
    return {(x, y): value[(x * ny + y) * BZ : (x * ny + y + 1) * BZ] for x in range(nx) for y in range(ny)}


def forward_kernel(own, x_even, x_odd, y_even_message, y_odd_message, y_even_ref, y_odd_ref, even_messages_ref, odd_messages_ref):
    even_y = lax.rem(lax.axis_index("ys"), 2) == 0
    lower, upper = [], []
    for ref, nx in ((own, BX), (x_even, REACH), (x_odd, REACH)):
        tiles = tiles_of(ref, 0, (nx, BY))
        lower += [tiles[x, y] for x in range(nx) for y in range(REACH)]
        upper += [tiles[x, y + BY - REACH] for x in range(nx) for y in range(REACH)]
    lower, upper = jnp.concatenate(lower, axis=0), jnp.concatenate(upper, axis=0)
    y_even_ref[:SLAB_Y] = jnp.where(even_y, upper, lower).astype(BF)
    y_odd_ref[:SLAB_Y] = jnp.where(even_y, lower, upper).astype(BF)
    y_even_ref[SLAB_Y:] = y_even_message[...]
    y_odd_ref[SLAB_Y:] = y_odd_message[...]
    for ref, at in ((even_messages_ref, 0), (odd_messages_ref, 2)):
        for i, source in enumerate((x_even, x_odd)):
            first = SLAB_X + at * LANES
            ref[i * LANES : (i + 1) * LANES] = source[first : first + LANES]


def forward(*operands):
    vmem = pl.BlockSpec(memory_space=pltpu.VMEM)
    return pl.pallas_call(
        forward_kernel,
        in_specs=[vmem] * 5,
        out_specs=[vmem] * 4,
        out_shape=[pltpu.VMEM((SLAB_Y + LANES, LANES), BF)] * 2 + [pltpu.VMEM((2 * LANES, LANES), BF)] * 2,
        compiler_params=pltpu.CompilerParams(vmem_limit_bytes=4 * 2**20),
        name="forward",
    )(*operands)


def sources_along_x(own, x_even, x_odd):
    even_x = lax.rem(lax.axis_index("xs"), 2) == 0
    found = {(REACH + x, REACH + y): t for (x, y), t in tiles_of(own, 0, (BX, BY)).items()}
    a, b = tiles_of(x_even, 0, (REACH, BY)), tiles_of(x_odd, 0, (REACH, BY))
    for x, y in a:
        found[x, REACH + y] = jnp.where(even_x, b[x, y], a[x, y])
        found[REACH + BX + x, REACH + y] = jnp.where(even_x, a[x, y], b[x, y])
    return found


def sources_along_y(y_even, y_odd):
    even_x = lax.rem(lax.axis_index("xs"), 2) == 0
    even_y = lax.rem(lax.axis_index("ys"), 2) == 0
    strips = []
    for ref in (y_even, y_odd):
        strip = {(REACH + x, y): t for (x, y), t in tiles_of(ref, 0, (BX, REACH)).items()}
        first = BX * REACH * BZ
        a = tiles_of(ref, first, (REACH, REACH))
        b = tiles_of(ref, first + REACH * REACH * BZ, (REACH, REACH))
        for x, y in a:
            strip[x, y] = jnp.where(even_x, b[x, y], a[x, y])
            strip[REACH + BX + x, y] = jnp.where(even_x, a[x, y], b[x, y])
        strips.append(strip)
    found = {}
    for x, y in strips[0]:
        found[x, y] = jnp.where(even_y, strips[1][x, y], strips[0][x, y])
        found[x, REACH + BY + y] = jnp.where(even_y, strips[0][x, y], strips[1][x, y])
    return found


def inner_kernel(own, x_even, x_odd, shifted_ref, grid_ref):
    for (x, y), box in sources_along_x(own, x_even, x_odd).items():
        grid_ref[x, y] = box
    shift_sources(INNER, grid_ref, shifted_ref)


def inner_pairs(own, x_even, x_odd):
    vmem = pl.BlockSpec(memory_space=pltpu.VMEM)
    return pl.pallas_call(
        inner_kernel,
        in_specs=[vmem] * 3,
        out_specs=[vmem] * 2,
        out_shape=[pltpu.VMEM((NSHIFT * len(INNER) * EXT, 16, LANES), BF), pltpu.VMEM((EXT, REACH + BY, BZ, LANES), F32)],
        compiler_params=pltpu.CompilerParams(vmem_limit_bytes=8 * 2**20),
        cost_estimate=pl.CostEstimate(flops=0, bytes_accessed=3 * 2**20, transcendentals=0),
        name="inner_pairs",
    )(own, x_even, x_odd)


def messages(x_even, x_odd, y_even, y_odd, even_passed, odd_passed):
    along_y = []
    for direct, passed in ((y_even, even_passed), (y_odd, odd_passed)):
        along_y += [(direct, SLAB_Y), (passed, 0), (passed, LANES)]
    return along_y + [(x_even, SLAB_X + LANES), (x_odd, SLAB_X + LANES)]


def m2l_kernel(inner, along_x, y_odd, y_even, first_ref, second_ref, local_ref, grid, outer):
    for (x, y), box in sources_along_y(y_even, y_odd).items():
        grid[x, y] = box
    for x in range(EXT):
        for y in (REACH, REACH + BY - 1):
            grid[x, y] = along_x[x, y]
    shift_sources(OUTER, grid, outer)
    listed = offsets()
    acc = jnp.zeros((LANES, LANES), F32)
    for k0 in range(0, len(listed), STEP):
        some = range(k0, min(k0 + STEP, len(listed)))
        a = [jnp.concatenate([first_ref[k], second_ref[k]], axis=0) for k in some]
        b = [shifted_sources(inner, outer, listed[k]) for k in some]
        acc = acc + nt(jnp.concatenate(a, axis=1), jnp.concatenate(b, axis=1))
    local_ref[...] = acc.astype(BF)


def m2l(inner, along_x, y_odd, y_even, first, second):
    vmem = pl.BlockSpec(memory_space=pltpu.VMEM)
    pinned = [pltpu.with_memory_space_constraint(x, pltpu.VMEM) for x in (inner, along_x, first, second)]
    return pl.pallas_call(
        m2l_kernel,
        in_specs=[vmem] * 6,
        out_specs=vmem,
        out_shape=jax.ShapeDtypeStruct((LANES, LANES), BF),
        scratch_shapes=[
            pltpu.VMEM((EXT, EXT, BZ, LANES), F32),
            pltpu.VMEM((NSHIFT * len(OUTER) * EXT, 16, LANES), BF),
        ],
        compiler_params=pltpu.CompilerParams(vmem_limit_bytes=16 * 2**20),
        cost_estimate=pl.CostEstimate(flops=0, bytes_accessed=2**16, transcendentals=0),
        name="m2l",
    )(pinned[0], pinned[1], y_odd, y_even, pinned[2], pinned[3])


def answer_kernel(terms, local_ref, x_odd, x_even, y_odd, y_even, odd_passed, even_passed, down_ref, up_ref, side_ref, tail_ref):
    local = local_ref[...]
    row = lax.broadcasted_iota(jnp.int32, (8, LANES), 0)
    answers = []
    for i, (ref, at) in enumerate(messages(x_even, x_odd, y_even, y_odd, even_passed, odd_passed)):
        x = ref[at : at + LANES, :].astype(F32)
        tail_ref[i : i + 1] = x[terms : terms + 1]
        tail_ref[8 + i : 9 + i] = x[terms + 1 : terms + 2]
        spread = one_hot(x[terms + 1 : terms + 2].astype(jnp.int32), LANES)
        column = jnp.dot(local, spread, preferred_element_type=F32)
        answers.append(jnp.sum(x[:terms] * column[:terms], axis=0, keepdims=True))
    for ref, first in ((down_ref, 0), (up_ref, 3), (side_ref, 6)):
        tile = jnp.zeros((8, LANES), F32)
        for i in range(min(3, 8 - first)):
            tile = jnp.where(row == i, answers[first + i], tile)
        ref[...] = tile


def answer(terms, *operands):
    vmem = pl.BlockSpec(memory_space=pltpu.VMEM)
    return pl.pallas_call(
        functools.partial(answer_kernel, terms),
        in_specs=[vmem] * 7,
        out_specs=[vmem] * 4,
        out_shape=[jax.ShapeDtypeStruct((8, LANES), F32)] * 3 + [jax.ShapeDtypeStruct((16, LANES), F32)],
        compiler_params=pltpu.CompilerParams(vmem_limit_bytes=4 * 2**20),
        name="answer",
    )(*operands)


def atoms_kernel(size_y, owner_ref, slot_ref, ion_ref, rows_ref, local_ref, tail_ref,
                 down_ref, up_ref, side_ref, local_exp_ref, far_ref, virial_ref):
    chunks = slot_ref.shape[0]
    local = local_ref[...]
    local_exp_ref[...] = local[: local_exp_ref.shape[0]]
    slots = jnp.where(owner_ref[...] == lax.axis_index("xs") * size_y + lax.axis_index("ys"), slot_ref[...], -1)
    row = lax.broadcasted_iota(jnp.int32, (8, LANES), 0)
    total = jnp.zeros((9 * 8, LANES), F32)
    for j in range(chunks):
        lanes = slice(j * LANES, (j + 1) * LANES)
        spread = one_hot(slots[j : j + 1], LANES)
        column = jnp.dot(local, spread, preferred_element_type=F32)
        far = jnp.zeros((8, LANES), F32)
        for f in range(FIELDS):
            value = jnp.sum(rows_ref[f, :, lanes].astype(F32) * column, axis=0, keepdims=True)
            far = jnp.where(row == f, value, far)
        far_ref[:, lanes] = far[:FIELDS]
        ion = ion_ref[j * FIELDS : (j + 1) * FIELDS, :].astype(F32)
        terms3 = jnp.concatenate([ion[0:1] * ion[a : a + 1] * far for a in (1, 2, 3)], axis=0)
        total = total + nt(split3(terms3), spread)

    per_peer = side_ref.shape[1] // FIELDS
    group = lax.broadcasted_iota(jnp.int32, (8, LANES), 1) // per_peer
    answers = [(down_ref, 0), (down_ref, 1), (down_ref, 2), (up_ref, 0), (up_ref, 1), (up_ref, 2), (side_ref, 0), (side_ref, 1)]
    for n, (answer, i) in enumerate(answers):
        d = AROUND.index(SENDERS[n])
        spread = one_hot(tail_ref[8 + n : 9 + n].astype(jnp.int32), LANES)
        ion = jnp.broadcast_to(tail_ref[n : n + 1], (8, LANES))

        def everywhere(f):
            x = jnp.where(group == (f + d) % FIELDS, ion, 0.0)
            x = x + pltpu.roll(x, 2 * per_peer, 1)
            return x + pltpu.roll(x, per_peer, 1)

        far = jnp.where(group == (row + d) % FIELDS, jnp.broadcast_to(answer[i : i + 1, :], (8, LANES)), 0.0)
        charge = everywhere(0)
        terms3 = jnp.concatenate([charge * everywhere(a) * far for a in (1, 2, 3)], axis=0)
        total = total + nt(split3(terms3), spread)
    virial = total[:24] + total[24:48] + total[48:]
    for a in range(3):
        virial_ref[3 * a : 3 * a + 3, :] = virial[8 * a + 1 : 8 * a + 4]


def atoms_of_device(terms, size_y, owner, slot, ions, rows, local, tail, down, up_, side):
    atoms = slot.shape[0]
    chunks = atoms // LANES
    whole = pl.BlockSpec(memory_space=pltpu.VMEM)
    ions = ions.reshape(FIELDS, chunks, LANES).transpose(1, 0, 2).reshape(FIELDS * chunks, LANES)
    return pl.pallas_call(
        functools.partial(atoms_kernel, size_y),
        in_specs=[whole] * 9,
        out_specs=[whole] * 3,
        out_shape=[jax.ShapeDtypeStruct((terms, LANES), BF), jax.ShapeDtypeStruct((FIELDS, atoms), F32),
                   jax.ShapeDtypeStruct((9, LANES), F32)],
        compiler_params=pltpu.CompilerParams(vmem_limit_bytes=16 * 2**20),
        cost_estimate=pl.CostEstimate(flops=4 * 10**6, bytes_accessed=8 * 2**20, transcendentals=0),
        name="atoms",
    )(owner.reshape(chunks, LANES), slot.reshape(chunks, LANES), ions, pltpu.with_memory_space_constraint(rows, pltpu.VMEM), local, tail, down, up_, side)


def turn_kernel(answer_x, y_even, y_odd, x_odd_ref, x_even_ref):
    for n, ref in ((1, x_even_ref), (2, x_odd_ref)):
        ref[...] = jnp.zeros(ref.shape, F32)
        ref[0:1] = answer_x[n - 1 : n]
        ref[1:2] = y_odd[n : n + 1]
        ref[2:3] = y_even[n : n + 1]


def turn(*operands):
    vmem = pl.BlockSpec(memory_space=pltpu.VMEM)
    return pl.pallas_call(
        turn_kernel,
        in_specs=[vmem] * 3,
        out_specs=[vmem] * 2,
        out_shape=[jax.ShapeDtypeStruct((8, LANES), F32)] * 2,
        compiler_params=pltpu.CompilerParams(vmem_limit_bytes=2**20),
        name="turn",
    )(*operands)


def merge_kernel(far_ref, place_ref, x_odd, x_even, y_odd, y_even, out_ref):
    per_peer = place_ref.shape[0] // 8
    each = LANES // per_peer
    returned = {
        (0, 1): (y_even, 0), (0, 2): (y_odd, 0),
        (1, 0): (x_even, 0), (1, 2): (x_even, 1), (1, 1): (x_even, 2),
        (2, 0): (x_odd, 0), (2, 2): (x_odd, 1), (2, 1): (x_odd, 2),
    }
    row = lax.broadcasted_iota(jnp.int32, (8, LANES), 0)
    group = lax.broadcasted_iota(jnp.int32, (8, LANES), 1) // per_peer
    halves = []
    for half in range(2):
        x = []
        for where in AROUND[half * each : half * each + each]:
            ref, i = returned[where]
            x.append(jnp.broadcast_to(ref[i : i + 1, :], (8, LANES)))
        tile = jnp.zeros((8, LANES), F32)
        for f in range(FIELDS):
            y = x[0]
            for g in range(1, each):
                y = jnp.where(group == (f + g) % each, x[g], y)
            tile = jnp.where(row == f, pltpu.roll(y, (each - f) * per_peer, 1) if f else y, tile)
        halves.append(tile)
    back = split3(jnp.concatenate(halves, axis=1))
    added = jnp.dot(back, place_ref[...], preferred_element_type=F32)
    out_ref[...] = far_ref[...] + (added[:FIELDS] + added[8 : 8 + FIELDS] + added[16 : 16 + FIELDS])


def merge(far, place, *returned):
    whole = pl.BlockSpec(memory_space=pltpu.VMEM)
    return pl.pallas_call(
        merge_kernel,
        in_specs=[whole] * 6,
        out_specs=whole,
        out_shape=jax.ShapeDtypeStruct(far.shape, F32),
        compiler_params=pltpu.CompilerParams(vmem_limit_bytes=16 * 2**20),
        name="merge",
    )(far, pltpu.with_memory_space_constraint(place, pltpu.VMEM), *returned)


def across(axis, edge, block):
    count = lax.axis_size(axis)
    pairs = [(i, (i + 1) % count) for i in range(edge - 1, count, 2)]
    return lax.ppermute(block, axis, pairs + [(b, a) for a, b in pairs])


def shards(
    multipoles,
    translation_ops,
    target_interaction_table,
    evaluation,
    ion_data,
    atom_owner,
    atom_slot,
):
    num_terms = multipoles.shape[0]
    size_x = lax.axis_size("xs")
    size_y = lax.axis_size("ys")
    own, to_x_even, to_x_odd, y_even_message, y_odd_message, rows, place = pack(
        (size_x, size_y), atom_owner, atom_slot, target_interaction_table, multipoles, evaluation, ion_data
    )
    x_even = across("xs", 1, to_x_even)
    x_odd = across("xs", 2, to_x_odd)
    first = by_operator(translation_ops, 0, 6)
    x_even, x_odd, first = lax.optimization_barrier((x_even, x_odd, first))
    to_y_even, to_y_odd, even_messages, odd_messages = forward(own, x_even, x_odd, y_even_message, y_odd_message)
    y_odd = across("ys", 2, to_y_odd)
    y_even = across("ys", 1, to_y_even)
    odd_messages = across("ys", 2, odd_messages)
    even_messages = across("ys", 1, even_messages)
    second = by_operator(translation_ops, 6, 2)
    inner, along_x = inner_pairs(own, x_even, x_odd)
    local = m2l(inner, along_x, y_odd, y_even, first, second)
    answer_y_even, answer_y_odd, answer_x, tail = answer(
        num_terms, local, x_odd, x_even, y_odd, y_even, odd_messages, even_messages
    )

    back_y_odd = across("ys", 2, answer_y_odd)
    back_y_even = across("ys", 1, answer_y_even)
    local_exp, far, box_virial = atoms_of_device(
        num_terms, size_y, atom_owner, atom_slot, ion_data, rows, local, tail, answer_y_even, answer_y_odd, answer_x
    )
    answer_x_odd, answer_x_even = turn(answer_x, back_y_even, back_y_odd)
    back_x_odd = across("xs", 2, answer_x_odd)
    back_x_even = across("xs", 1, answer_x_even)
    atom_far_field = merge(far, place, back_x_odd, back_x_even, back_y_odd, back_y_even)
    return (local_exp, atom_far_field, box_virial)


def solution(mesh):
    placed = (
        P(None, ("xs", "ys")),
        P(),
        P(None, ("xs", "ys")),
        P(None, None, ("xs", "ys")),
        P(None, ("xs", "ys")),
        P(("xs", "ys"), None),
        P(("xs", "ys")),
    )
    return jax.shard_map(
        shards,
        mesh=mesh,
        in_specs=placed,
        out_specs=(P(None, ("xs", "ys")), P(None, ("xs", "ys")), P(None, ("xs", "ys"))),
        check_vma=False,
    )
```

```python
import functools

import jax
import jax.numpy as jnp
from jax import lax
from jax.experimental import pallas as pl
from jax.experimental.pallas import tpu as pltpu
from jax.sharding import PartitionSpec as P

BF = jnp.bfloat16
F32 = jnp.float32
REACH = 3
NSHIFT = 2 * REACH + 1
LANES = 128
BX = 4
BY = 4
BZ = 8
EXT = BX + 2 * REACH
SLAB_X = REACH * BY * BZ
SLAB_Y = BX * REACH * BZ + 2 * REACH * REACH * BZ
FIELDS = 4
STEP = 316
AROUND = [(1, 1), (1, 0), (1, 2), (2, 1), (2, 0), (2, 2), (0, 1), (0, 2)]
SENDERS = [(1, 0), (1, 1), (1, 2), (2, 0), (2, 1), (2, 2), (0, 1), (0, 2)]


def offsets():
    listed = []
    for dx in range(-REACH, REACH + 1):
        for dy in range(-REACH, REACH + 1):
            for dz in range(-REACH, REACH + 1):
                if max(abs(dx), abs(dy), abs(dz)) >= 2:
                    listed.append((dx, dy, dz))
    return listed


def up(value, unit):
    return -(-value // unit) * unit


def by_operator_kernel(first, ops_ref, out_ref, held, sems):
    terms, noff, _ = ops_ref.shape
    total = out_ref.shape[0]
    part = up(total // 4, 16)
    cuts = [slice(k, min(k + part, noff)) for k in range(0, noff, part)]
    copies = {}
    for j in range(held.shape[0]):
        q = (first + j) * 16
        some = min(16, terms - q)
        for n, cut in enumerate(cuts if j == 0 else [slice(0, noff)]):
            copies[j, cut.start] = pltpu.make_async_copy(
                ops_ref.at[q : q + some, cut, :], held.at[j, :some, cut, :], sems.at[n if j == 0 else j + len(cuts) - 1]
            )
            copies[j, cut.start].start()
    for j in range(held.shape[0]):
        some = min(16, terms - (first + j) * 16)
        rows = slice(16 * j, 16 * j + 16)
        for k0 in range(0, total, 16):
            if (j, k0) in copies:
                copies[j, k0].wait()
            x = held[j, :some, k0 : min(k0 + 16, noff), :]
            if k0 + 16 > noff:
                x = jnp.concatenate([x.astype(F32), jnp.zeros((some, k0 + 16 - noff, terms), F32)], axis=1).astype(BF)
            if some < 16:
                x = jnp.concatenate([x, jnp.zeros((16 - some, 16, terms), BF)], axis=0)
            x = jnp.concatenate([x, jnp.zeros((16, 16, LANES - terms), BF)], axis=2)
            out_ref[k0 : k0 + 16, rows, :] = jnp.swapaxes(x, 0, 1)


def by_operator(ops, first, steps):
    noff, terms, _ = ops.shape
    total = up(noff, 16)
    return pl.pallas_call(
        functools.partial(by_operator_kernel, first),
        in_specs=[pl.BlockSpec(memory_space=pl.ANY)],
        out_specs=pl.BlockSpec(memory_space=pltpu.VMEM),
        out_shape=pltpu.VMEM((total, steps * 16, LANES), BF),
        scratch_shapes=[pltpu.VMEM((steps, 16, noff, terms), BF), pltpu.SemaphoreType.DMA((steps + 3,))],
        compiler_params=pltpu.CompilerParams(vmem_limit_bytes=16 * 2**20),
        cost_estimate=pl.CostEstimate(flops=0, bytes_accessed=2 * total * steps * 16 * LANES * 2, transcendentals=0),
        name="by_operator",
    )(pltpu.with_memory_space_constraint(jnp.transpose(ops, (1, 0, 2)), pltpu.HBM))


INNER = [(3, None), (4, None), (5, None), (2, 1), (6, 0)]
OUTER = [(1, None), (2, None), (6, None), (7, None), (0, 1), (8, 0)]


def shift_sources(pairs, grid, out_ref):
    parity = lax.broadcasted_iota(jnp.int32, (BZ, LANES), 0) % 2
    nothing = jnp.zeros((BZ, LANES), F32)
    for dz in range(-REACH, REACH + 1):
        for x in range(EXT):
            turned = {}

            def tile(y):
                if y not in turned:
                    t = grid[x, y]
                    if dz:
                        t = pltpu.roll(t, (-dz) % BZ, 0)
                    if abs(dz) == REACH:
                        t = jnp.where(parity == (0 if dz > 0 else 1), t, 0.0)
                    turned[y] = t
                return turned[y]

            for n, (y, keep) in enumerate(pairs):
                halves = [tile(y + i) if keep in (None, i) else nothing for i in range(2)]
                out_ref[((dz + REACH) * len(pairs) + n) * EXT + x] = jnp.concatenate(halves, axis=0).astype(BF)


def shifted_sources(inner, outer, offset):
    dx, dy, dz = offset
    tiles = []
    for bx in range(BX):
        for h in range(2):
            pair = (dy + REACH + 2 * h, {-REACH: 1, REACH: 0}.get(dy))
            ref, pairs = (inner, INNER) if pair in INNER else (outer, OUTER)
            if abs(dx) == REACH and bx % 2 != (0 if dx > 0 else 1):
                tiles.append(jnp.zeros((16, LANES), BF))
            else:
                tiles.append(ref[((dz + REACH) * len(pairs) + pairs.index(pair)) * EXT + REACH + dx + bx])
    return jnp.concatenate(tiles, axis=0)


def one_hot(index, rows):
    at = lax.broadcasted_iota(jnp.int32, (rows, index.shape[1]), 0)
    return (at == index).astype(F32).astype(BF)


def split3(x):
    high = x.astype(BF).astype(F32)
    middle = (x - high).astype(BF).astype(F32)
    return jnp.concatenate([high, middle, x - high - middle], axis=0).astype(BF)


def nt(a, b):
    return lax.dot_general(a, b, (((1,), (1,)), ((), ())), preferred_element_type=F32)


def neighbours(size_x, size_y):
    ix, iy = lax.axis_index("xs"), lax.axis_index("ys")
    step_x = [0, 1 - 2 * lax.rem(ix, 2), 2 * lax.rem(ix, 2) - 1]
    step_y = [0, 1 - 2 * lax.rem(iy, 2), 2 * lax.rem(iy, 2) - 1]
    return [
        lax.rem(ix + step_x[x] + size_x, size_x) * size_y + lax.rem(iy + step_y[y] + size_y, size_y)
        for x, y in AROUND
    ]


def pack_kernel(sizes, owner_hbm, slot_hbm, table_hbm, multipoles_hbm, evaluation_ref, ion_hbm,
                own_ref, x_even_ref, x_odd_ref, y_even_ref, y_odd_ref, rows_ref, place_ref,
                held, owner_ref, slot_ref, table_ref, multipoles_ref, ion_ref, sems):
    terms = multipoles_ref.shape[0]
    groups = held.shape[0]
    above = offsets().index((0, 0, 2))
    small = [(table_hbm.at[above // 8 * 8 : above // 8 * 8 + 8, :], table_ref), (multipoles_hbm, multipoles_ref),
             (owner_hbm, owner_ref), (slot_hbm, slot_ref), (ion_hbm, ion_ref)]
    copies = [pltpu.make_async_copy(evaluation_ref.at[:, 16 * j : 16 * j + 16, :], held.at[j], sems.at[j])
              for j in range(groups)]
    copies += [pltpu.make_async_copy(a, b, sems.at[groups + i]) for i, (a, b) in enumerate(small)]
    for copy in copies[groups:] + copies[:groups]:
        copy.start()
    for copy in copies[groups:]:
        copy.wait()
    chunks = slot_ref.shape[0]
    per_peer = place_ref.shape[0] // 8
    row = table_ref[above % 8 : above % 8 + 1, :]
    z = lax.broadcasted_iota(jnp.int32, row.shape, 1) % BZ
    row = jnp.where(z >= 2, pltpu.roll(row, 2, 1), pltpu.roll(row, LANES - 6, 1))
    masked = jnp.where(row >= 0, multipoles_ref[...].astype(F32), 0.0)
    masked = jnp.concatenate([masked, jnp.zeros((LANES - terms, LANES), F32)], axis=0).T
    own_ref[...] = masked.astype(BF)
    even_x = lax.rem(lax.axis_index("xs"), 2) == 0
    lower, upper = masked[:SLAB_X], masked[LANES - SLAB_X :]
    x_even_ref[:SLAB_X] = jnp.where(even_x, upper, lower).astype(BF)
    x_odd_ref[:SLAB_X] = jnp.where(even_x, lower, upper).astype(BF)

    owner = owner_ref[...]
    member = [(owner == device).astype(F32) for device in neighbours(*sizes)]
    stacked = jnp.concatenate(member, axis=0).astype(BF)
    n = 8 * chunks
    r = lax.broadcasted_iota(jnp.int32, (n, n), 0)
    c = lax.broadcasted_iota(jnp.int32, (n, n), 1)
    earlier = ((r // chunks == c // chunks) & (c < r)).astype(F32).astype(BF)
    r = lax.broadcasted_iota(jnp.int32, (LANES, LANES), 0)
    c = lax.broadcasted_iota(jnp.int32, (LANES, LANES), 1)
    before = (r < c).astype(F32).astype(BF)
    ones = jnp.ones((LANES, LANES), BF)
    ahead = jnp.dot(earlier, stacked, preferred_element_type=F32).astype(BF)
    rank = jnp.dot(stacked, before, preferred_element_type=F32) + jnp.dot(ahead, ones, preferred_element_type=F32)
    place = jnp.full((chunks, LANES), -1.0, F32)
    for d in range(8):
        place = jnp.where(member[d] > 0, rank[d * chunks : (d + 1) * chunks] + d * per_peer, place)
    place = place.astype(jnp.int32)
    for j in range(chunks):
        place_ref[:, j * LANES : (j + 1) * LANES] = one_hot(place[j : j + 1], 8 * per_peer)

    half_way = groups // 2 * 4 * LANES

    def picked_by(first, last):
        x = rows_ref[:, :, first:last].reshape(FIELDS * LANES, last - first)
        return nt(x, place_ref[:, first:last])

    slot = slot_ref[...].astype(F32)
    for j in range(chunks // 4):
        part = slice(16 * j, 16 * j + 16)
        if j == groups // 2:
            picked = picked_by(0, half_way)
        slots = [jnp.broadcast_to(slot[4 * j + i : 4 * j + i + 1], (4, LANES)) for i in range(4)]
        extra = [ion_ref[part, :], jnp.concatenate(slots, axis=0).astype(BF)]
        extra = jnp.concatenate([e.reshape(1, 16, LANES) for e in extra], axis=0)
        copies[j].wait()
        for p in range(0, LANES, 16):
            x = held[j, p : min(p + 16, terms)]
            if p + 16 > terms:
                x = jnp.concatenate([x, extra, jnp.zeros((16 - x.shape[0] - 2, 16, LANES), BF)], axis=0)
            x = jnp.swapaxes(x, 0, 1)
            for i in range(4):
                lanes = slice((4 * j + i) * LANES, (4 * j + i + 1) * LANES)
                for f in range(FIELDS):
                    rows_ref[f, p : p + 16, lanes] = x[4 * i + f]

    picked = picked + picked_by(half_way, place_ref.shape[1])

    targets = {
        (1, 1): (x_even_ref, 0), (1, 0): (x_even_ref, 1), (1, 2): (x_even_ref, 2),
        (2, 1): (x_odd_ref, 0), (2, 0): (x_odd_ref, 1), (2, 2): (x_odd_ref, 2),
        (0, 1): (y_even_ref, 0), (0, 2): (y_odd_ref, 0),
    }
    lane = lax.broadcasted_iota(jnp.int32, (LANES, LANES), 1) // per_peer
    each = LANES // per_peer
    turned = []
    for half in range(2):
        x = [picked[f * LANES : (f + 1) * LANES, half * LANES : (half + 1) * LANES] for f in range(FIELDS)]
        turned.append([pltpu.roll(t, f * per_peer, 1) if f else t for f, t in enumerate(x)])
    for d, where in enumerate(AROUND):
        message = turned[d // each][0]
        for f in range(1, FIELDS):
            message = jnp.where(lane == (f + d) % each, turned[d // each][f], message)
        ref, at = targets[where]
        at = at * LANES + (SLAB_X if where[0] else 0)
        ref[at : at + LANES] = message.astype(BF)


def pack(sizes, owner, slot, table, multipoles, evaluation, ions):
    terms = multipoles.shape[0]
    atoms = slot.shape[0]
    chunks = atoms // LANES
    per_peer = atoms // 64
    whole = pl.BlockSpec(memory_space=pltpu.VMEM)
    view = evaluation.transpose(1, 0, 2).reshape(terms, FIELDS, chunks, LANES)
    view = view.transpose(0, 2, 1, 3).reshape(terms, FIELDS * chunks, LANES)
    ions = ions.reshape(FIELDS, chunks, LANES).transpose(1, 0, 2).reshape(FIELDS * chunks, LANES)
    block = lambda rows: jax.ShapeDtypeStruct((rows, LANES), BF)
    return pl.pallas_call(
        functools.partial(pack_kernel, sizes),
        in_specs=[pl.BlockSpec(memory_space=pl.ANY)] * 6,
        out_specs=[whole] * 7,
        out_shape=[block(LANES), block(SLAB_X + 3 * LANES), block(SLAB_X + 3 * LANES), block(LANES), block(LANES),
                   pltpu.VMEM((FIELDS, LANES, atoms), BF),
                   pltpu.VMEM((8 * per_peer, atoms), BF)],
        scratch_shapes=[
            pltpu.VMEM((chunks // 4, terms, 16, LANES), BF),
            pltpu.VMEM((chunks, LANES), jnp.int32),
            pltpu.VMEM((chunks, LANES), jnp.int32),
            pltpu.VMEM((8, LANES), jnp.int32),
            pltpu.VMEM((terms, LANES), BF),
            pltpu.VMEM((FIELDS * chunks, LANES), BF),
            pltpu.SemaphoreType.DMA((chunks // 4 + 5,)),
        ],
        compiler_params=pltpu.CompilerParams(vmem_limit_bytes=24 * 2**20),
        name="pack",
    )(*(pltpu.with_memory_space_constraint(x, pltpu.HBM) for x in (
        owner.reshape(chunks, LANES), slot.reshape(chunks, LANES), table, multipoles, view, ions)))


def tiles_of(ref, first, shape):
    nx, ny = shape
    value = ref[first : first + nx * ny * BZ, :].astype(F32)
    return {(x, y): value[(x * ny + y) * BZ : (x * ny + y + 1) * BZ] for x in range(nx) for y in range(ny)}


def forward_kernel(own, x_even, x_odd, y_even_message, y_odd_message, y_even_ref, y_odd_ref, even_messages_ref, odd_messages_ref):
    even_y = lax.rem(lax.axis_index("ys"), 2) == 0
    lower, upper = [], []
    for ref, nx in ((own, BX), (x_even, REACH), (x_odd, REACH)):
        tiles = tiles_of(ref, 0, (nx, BY))
        lower += [tiles[x, y] for x in range(nx) for y in range(REACH)]
        upper += [tiles[x, y + BY - REACH] for x in range(nx) for y in range(REACH)]
    lower, upper = jnp.concatenate(lower, axis=0), jnp.concatenate(upper, axis=0)
    y_even_ref[:SLAB_Y] = jnp.where(even_y, upper, lower).astype(BF)
    y_odd_ref[:SLAB_Y] = jnp.where(even_y, lower, upper).astype(BF)
    y_even_ref[SLAB_Y:] = y_even_message[...]
    y_odd_ref[SLAB_Y:] = y_odd_message[...]
    for ref, at in ((even_messages_ref, 0), (odd_messages_ref, 2)):
        for i, source in enumerate((x_even, x_odd)):
            first = SLAB_X + at * LANES
            ref[i * LANES : (i + 1) * LANES] = source[first : first + LANES]


def forward(*operands):
    vmem = pl.BlockSpec(memory_space=pltpu.VMEM)
    return pl.pallas_call(
        forward_kernel,
        in_specs=[vmem] * 5,
        out_specs=[vmem] * 4,
        out_shape=[pltpu.VMEM((SLAB_Y + LANES, LANES), BF)] * 2 + [pltpu.VMEM((2 * LANES, LANES), BF)] * 2,
        compiler_params=pltpu.CompilerParams(vmem_limit_bytes=4 * 2**20),
        name="forward",
    )(*operands)


def sources_along_x(own, x_even, x_odd):
    even_x = lax.rem(lax.axis_index("xs"), 2) == 0
    found = {(REACH + x, REACH + y): t for (x, y), t in tiles_of(own, 0, (BX, BY)).items()}
    a, b = tiles_of(x_even, 0, (REACH, BY)), tiles_of(x_odd, 0, (REACH, BY))
    for x, y in a:
        found[x, REACH + y] = jnp.where(even_x, b[x, y], a[x, y])
        found[REACH + BX + x, REACH + y] = jnp.where(even_x, a[x, y], b[x, y])
    return found


def sources_along_y(y_even, y_odd):
    even_x = lax.rem(lax.axis_index("xs"), 2) == 0
    even_y = lax.rem(lax.axis_index("ys"), 2) == 0
    strips = []
    for ref in (y_even, y_odd):
        strip = {(REACH + x, y): t for (x, y), t in tiles_of(ref, 0, (BX, REACH)).items()}
        first = BX * REACH * BZ
        a = tiles_of(ref, first, (REACH, REACH))
        b = tiles_of(ref, first + REACH * REACH * BZ, (REACH, REACH))
        for x, y in a:
            strip[x, y] = jnp.where(even_x, b[x, y], a[x, y])
            strip[REACH + BX + x, y] = jnp.where(even_x, a[x, y], b[x, y])
        strips.append(strip)
    found = {}
    for x, y in strips[0]:
        found[x, y] = jnp.where(even_y, strips[1][x, y], strips[0][x, y])
        found[x, REACH + BY + y] = jnp.where(even_y, strips[0][x, y], strips[1][x, y])
    return found


def inner_kernel(own, x_even, x_odd, shifted_ref, grid_ref):
    for (x, y), box in sources_along_x(own, x_even, x_odd).items():
        grid_ref[x, y] = box
    shift_sources(INNER, grid_ref, shifted_ref)


def inner_pairs(own, x_even, x_odd):
    vmem = pl.BlockSpec(memory_space=pltpu.VMEM)
    return pl.pallas_call(
        inner_kernel,
        in_specs=[vmem] * 3,
        out_specs=[vmem] * 2,
        out_shape=[pltpu.VMEM((NSHIFT * len(INNER) * EXT, 16, LANES), BF), pltpu.VMEM((EXT, REACH + BY, BZ, LANES), F32)],
        compiler_params=pltpu.CompilerParams(vmem_limit_bytes=8 * 2**20),
        cost_estimate=pl.CostEstimate(flops=0, bytes_accessed=3 * 2**20, transcendentals=0),
        name="inner_pairs",
    )(own, x_even, x_odd)


def messages(x_even, x_odd, y_even, y_odd, even_passed, odd_passed):
    direct = SLAB_X + LANES
    return [
        (x_even, direct), (even_passed, 0), (odd_passed, 0), (x_odd, direct), (even_passed, LANES), (odd_passed, LANES),
        (y_even, SLAB_Y), (y_odd, SLAB_Y),
    ]


def m2l_kernel(inner, along_x, y_odd, y_even, first_ref, second_ref, local_ref, grid, outer):
    for (x, y), box in sources_along_y(y_even, y_odd).items():
        grid[x, y] = box
    for x in range(EXT):
        for y in (REACH, REACH + BY - 1):
            grid[x, y] = along_x[x, y]
    shift_sources(OUTER, grid, outer)
    listed = offsets()
    acc = jnp.zeros((LANES, LANES), F32)
    for k0 in range(0, len(listed), STEP):
        some = range(k0, min(k0 + STEP, len(listed)))
        a = [jnp.concatenate([first_ref[k], second_ref[k]], axis=0) for k in some]
        b = [shifted_sources(inner, outer, listed[k]) for k in some]
        acc = acc + nt(jnp.concatenate(a, axis=1), jnp.concatenate(b, axis=1))
    local_ref[...] = acc.astype(BF)


def m2l(inner, along_x, y_odd, y_even, first, second):
    vmem = pl.BlockSpec(memory_space=pltpu.VMEM)
    pinned = [pltpu.with_memory_space_constraint(x, pltpu.VMEM) for x in (inner, along_x, first, second)]
    return pl.pallas_call(
        m2l_kernel,
        in_specs=[vmem] * 6,
        out_specs=vmem,
        out_shape=jax.ShapeDtypeStruct((LANES, LANES), BF),
        scratch_shapes=[
            pltpu.VMEM((EXT, EXT, BZ, LANES), F32),
            pltpu.VMEM((NSHIFT * len(OUTER) * EXT, 16, LANES), BF),
        ],
        compiler_params=pltpu.CompilerParams(vmem_limit_bytes=16 * 2**20),
        cost_estimate=pl.CostEstimate(flops=0, bytes_accessed=2**16, transcendentals=0),
        name="m2l",
    )(pinned[0], pinned[1], y_odd, y_even, pinned[2], pinned[3])


def answer_kernel(terms, local_ref, x_odd, x_even, y_odd, y_even, odd_passed, even_passed, by_even_ref, by_odd_ref, by_y_ref, tail_ref):
    local = local_ref[...]
    row = lax.broadcasted_iota(jnp.int32, (8, LANES), 0)
    answers = []
    for i, (ref, at) in enumerate(messages(x_even, x_odd, y_even, y_odd, even_passed, odd_passed)):
        x = ref[at : at + LANES, :].astype(F32)
        tail_ref[i : i + 1] = x[terms : terms + 1]
        tail_ref[8 + i : 9 + i] = x[terms + 1 : terms + 2]
        spread = one_hot(x[terms + 1 : terms + 2].astype(jnp.int32), LANES)
        column = jnp.dot(local, spread, preferred_element_type=F32)
        answers.append(jnp.sum(x[:terms] * column[:terms], axis=0, keepdims=True))
    for ref, first in ((by_even_ref, 0), (by_odd_ref, 3), (by_y_ref, 6)):
        tile = jnp.zeros((8, LANES), F32)
        for i in range(min(3, 8 - first)):
            tile = jnp.where(row == i, answers[first + i], tile)
        ref[...] = tile


def answer(terms, *operands):
    vmem = pl.BlockSpec(memory_space=pltpu.VMEM)
    return pl.pallas_call(
        functools.partial(answer_kernel, terms),
        in_specs=[vmem] * 7,
        out_specs=[vmem] * 4,
        out_shape=[jax.ShapeDtypeStruct((8, LANES), F32)] * 3 + [jax.ShapeDtypeStruct((16, LANES), F32)],
        compiler_params=pltpu.CompilerParams(vmem_limit_bytes=4 * 2**20),
        name="answer",
    )(*operands)


def atoms_kernel(size_y, owner_ref, slot_ref, ion_ref, rows_ref, local_ref, tail_ref,
                 by_even_ref, by_odd_ref, by_y_ref, local_exp_ref, far_ref, virial_ref):
    chunks = slot_ref.shape[0]
    local = local_ref[...]
    local_exp_ref[...] = local[: local_exp_ref.shape[0]]
    slots = jnp.where(owner_ref[...] == lax.axis_index("xs") * size_y + lax.axis_index("ys"), slot_ref[...], -1)
    row = lax.broadcasted_iota(jnp.int32, (8, LANES), 0)
    total = jnp.zeros((9 * 8, LANES), F32)
    for j in range(chunks):
        lanes = slice(j * LANES, (j + 1) * LANES)
        spread = one_hot(slots[j : j + 1], LANES)
        column = jnp.dot(local, spread, preferred_element_type=F32)
        far = jnp.zeros((8, LANES), F32)
        for f in range(FIELDS):
            value = jnp.sum(rows_ref[f, :, lanes].astype(F32) * column, axis=0, keepdims=True)
            far = jnp.where(row == f, value, far)
        far_ref[:, lanes] = far[:FIELDS]
        ion = ion_ref[j * FIELDS : (j + 1) * FIELDS, :].astype(F32)
        terms3 = jnp.concatenate([ion[0:1] * ion[a : a + 1] * far for a in (1, 2, 3)], axis=0)
        total = total + nt(split3(terms3), spread)

    per_peer = by_y_ref.shape[1] // FIELDS
    group = lax.broadcasted_iota(jnp.int32, (8, LANES), 1) // per_peer
    answers = [(ref, i) for ref in (by_even_ref, by_odd_ref) for i in range(3)] + [(by_y_ref, 0), (by_y_ref, 1)]
    for n, (answer, i) in enumerate(answers):
        d = AROUND.index(SENDERS[n])
        spread = one_hot(tail_ref[8 + n : 9 + n].astype(jnp.int32), LANES)
        ion = jnp.broadcast_to(tail_ref[n : n + 1], (8, LANES))

        def everywhere(f):
            x = jnp.where(group == (f + d) % FIELDS, ion, 0.0)
            x = x + pltpu.roll(x, 2 * per_peer, 1)
            return x + pltpu.roll(x, per_peer, 1)

        far = jnp.where(group == (row + d) % FIELDS, jnp.broadcast_to(answer[i : i + 1, :], (8, LANES)), 0.0)
        charge = everywhere(0)
        terms3 = jnp.concatenate([charge * everywhere(a) * far for a in (1, 2, 3)], axis=0)
        total = total + nt(split3(terms3), spread)
    virial = total[:24] + total[24:48] + total[48:]
    for a in range(3):
        virial_ref[3 * a : 3 * a + 3, :] = virial[8 * a + 1 : 8 * a + 4]


def atoms_of_device(terms, size_y, owner, slot, ions, rows, local, tail, down, up_, side):
    atoms = slot.shape[0]
    chunks = atoms // LANES
    whole = pl.BlockSpec(memory_space=pltpu.VMEM)
    ions = ions.reshape(FIELDS, chunks, LANES).transpose(1, 0, 2).reshape(FIELDS * chunks, LANES)
    return pl.pallas_call(
        functools.partial(atoms_kernel, size_y),
        in_specs=[whole] * 9,
        out_specs=[whole] * 3,
        out_shape=[jax.ShapeDtypeStruct((terms, LANES), BF), jax.ShapeDtypeStruct((FIELDS, atoms), F32),
                   jax.ShapeDtypeStruct((9, LANES), F32)],
        compiler_params=pltpu.CompilerParams(vmem_limit_bytes=16 * 2**20),
        cost_estimate=pl.CostEstimate(flops=4 * 10**6, bytes_accessed=8 * 2**20, transcendentals=0),
        name="atoms",
    )(owner.reshape(chunks, LANES), slot.reshape(chunks, LANES), ions, pltpu.with_memory_space_constraint(rows, pltpu.VMEM), local, tail, down, up_, side)


def turn_kernel(answer_y, x_even, x_odd, y_odd_ref, y_even_ref):
    for n, ref in ((1, y_even_ref), (2, y_odd_ref)):
        ref[...] = jnp.zeros(ref.shape, F32)
        ref[0:1] = answer_y[n - 1 : n]
        ref[1:2] = x_even[n : n + 1]
        ref[2:3] = x_odd[n : n + 1]


def turn(*operands):
    vmem = pl.BlockSpec(memory_space=pltpu.VMEM)
    return pl.pallas_call(
        turn_kernel,
        in_specs=[vmem] * 3,
        out_specs=[vmem] * 2,
        out_shape=[jax.ShapeDtypeStruct((8, LANES), F32)] * 2,
        compiler_params=pltpu.CompilerParams(vmem_limit_bytes=2**20),
        name="turn",
    )(*operands)


def merge_kernel(far_ref, place_ref, x_odd, x_even, y_odd, y_even, out_ref):
    per_peer = place_ref.shape[0] // 8
    each = LANES // per_peer
    returned = {
        (1, 0): (x_even, 0), (2, 0): (x_odd, 0),
        (0, 1): (y_even, 0), (1, 1): (y_even, 1), (2, 1): (y_even, 2),
        (0, 2): (y_odd, 0), (1, 2): (y_odd, 1), (2, 2): (y_odd, 2),
    }
    row = lax.broadcasted_iota(jnp.int32, (8, LANES), 0)
    group = lax.broadcasted_iota(jnp.int32, (8, LANES), 1) // per_peer
    halves = []
    for half in range(2):
        x = []
        for where in AROUND[half * each : half * each + each]:
            ref, i = returned[where]
            x.append(jnp.broadcast_to(ref[i : i + 1, :], (8, LANES)))
        tile = jnp.zeros((8, LANES), F32)
        for f in range(FIELDS):
            y = x[0]
            for g in range(1, each):
                y = jnp.where(group == (f + g) % each, x[g], y)
            tile = jnp.where(row == f, pltpu.roll(y, (each - f) * per_peer, 1) if f else y, tile)
        halves.append(tile)
    back = split3(jnp.concatenate(halves, axis=1))
    added = jnp.dot(back, place_ref[...], preferred_element_type=F32)
    out_ref[...] = far_ref[...] + (added[:FIELDS] + added[8 : 8 + FIELDS] + added[16 : 16 + FIELDS])


def merge(far, place, *returned):
    whole = pl.BlockSpec(memory_space=pltpu.VMEM)
    return pl.pallas_call(
        merge_kernel,
        in_specs=[whole] * 6,
        out_specs=whole,
        out_shape=jax.ShapeDtypeStruct(far.shape, F32),
        compiler_params=pltpu.CompilerParams(vmem_limit_bytes=16 * 2**20),
        name="merge",
    )(far, pltpu.with_memory_space_constraint(place, pltpu.VMEM), *returned)


def across(axis, edge, block):
    count = lax.axis_size(axis)
    pairs = [(i, (i + 1) % count) for i in range(edge - 1, count, 2)]
    return lax.ppermute(block, axis, pairs + [(b, a) for a, b in pairs])


def shards(
    multipoles,
    translation_ops,
    target_interaction_table,
    evaluation,
    ion_data,
    atom_owner,
    atom_slot,
):
    num_terms = multipoles.shape[0]
    size_x = lax.axis_size("xs")
    size_y = lax.axis_size("ys")
    own, to_x_even, to_x_odd, y_even_message, y_odd_message, rows, place = pack(
        (size_x, size_y), atom_owner, atom_slot, target_interaction_table, multipoles, evaluation, ion_data
    )
    x_even = across("xs", 1, to_x_even)
    x_odd = across("xs", 2, to_x_odd)
    first = by_operator(translation_ops, 0, 6)
    x_even, x_odd, first = lax.optimization_barrier((x_even, x_odd, first))
    to_y_even, to_y_odd, even_messages, odd_messages = forward(own, x_even, x_odd, y_even_message, y_odd_message)
    y_odd = across("ys", 2, to_y_odd)
    y_even = across("ys", 1, to_y_even)
    odd_messages = across("ys", 2, odd_messages)
    even_messages = across("ys", 1, even_messages)
    second = by_operator(translation_ops, 6, 2)
    inner, along_x = inner_pairs(own, x_even, x_odd)
    local = m2l(inner, along_x, y_odd, y_even, first, second)
    answer_x_even, answer_x_odd, answer_y, tail = answer(
        num_terms, local, x_odd, x_even, y_odd, y_even, odd_messages, even_messages
    )

    back_x_even = across("xs", 1, answer_x_even)
    back_x_odd = across("xs", 2, answer_x_odd)
    local_exp, far, box_virial = atoms_of_device(
        num_terms, size_y, atom_owner, atom_slot, ion_data, rows, local, tail, answer_x_even, answer_x_odd, answer_y
    )
    back_x_even, back_x_odd, far = lax.optimization_barrier((back_x_even, back_x_odd, far))
    answer_y_odd, answer_y_even = turn(answer_y, back_x_even, back_x_odd)
    back_y_odd = across("ys", 2, answer_y_odd)
    back_y_even = across("ys", 1, answer_y_even)
    atom_far_field = merge(far, place, back_x_odd, back_x_even, back_y_odd, back_y_even)
    return (local_exp, atom_far_field, box_virial)


def solution(mesh):
    placed = (
        P(None, ("xs", "ys")),
        P(),
        P(None, ("xs", "ys")),
        P(None, None, ("xs", "ys")),
        P(None, ("xs", "ys")),
        P(("xs", "ys"), None),
        P(("xs", "ys")),
    )
    return jax.shard_map(
        shards,
        mesh=mesh,
        in_specs=placed,
        out_specs=(P(None, ("xs", "ys")), P(None, ("xs", "ys")), P(None, ("xs", "ys"))),
        check_vma=False,
    )
```

```python
import functools

import jax
import jax.numpy as jnp
from jax import lax
from jax.experimental import pallas as pl
from jax.experimental.pallas import tpu as pltpu
from jax.sharding import PartitionSpec as P

BF = jnp.bfloat16
F32 = jnp.float32
REACH = 3
NSHIFT = 2 * REACH + 1
LANES = 128
BX = 4
BY = 4
BZ = 8
EXT = BX + 2 * REACH
SLAB_X = REACH * BY * BZ
SLAB_Y = BX * REACH * BZ + 2 * REACH * REACH * BZ
FIELDS = 4
STEP = 40
AROUND = [(1, 1), (1, 0), (1, 2), (2, 1), (2, 0), (2, 2), (0, 1), (0, 2)]
SENDERS = [(1, 0), (1, 1), (1, 2), (2, 0), (2, 1), (2, 2), (0, 1), (0, 2)]


def offsets():
    listed = []
    for dx in range(-REACH, REACH + 1):
        for dy in range(-REACH, REACH + 1):
            for dz in range(-REACH, REACH + 1):
                if max(abs(dx), abs(dy), abs(dz)) >= 2:
                    listed.append((dx, dy, dz))
    return listed


def up(value, unit):
    return -(-value // unit) * unit


def by_operator_kernel(first, ops_ref, out_ref, held, sems):
    terms, noff, _ = ops_ref.shape
    total = out_ref.shape[0]
    part = up(total // 4, 16)
    cuts = [slice(k, min(k + part, noff)) for k in range(0, noff, part)]
    copies = {}
    for j in range(held.shape[0]):
        q = (first + j) * 16
        some = min(16, terms - q)
        for n, cut in enumerate(cuts if j == 0 else [slice(0, noff)]):
            copies[j, cut.start] = pltpu.make_async_copy(
                ops_ref.at[q : q + some, cut, :], held.at[j, :some, cut, :], sems.at[n if j == 0 else j + len(cuts) - 1]
            )
            copies[j, cut.start].start()
    for j in range(held.shape[0]):
        some = min(16, terms - (first + j) * 16)
        rows = slice(16 * j, 16 * j + 16)
        for k0 in range(0, total, 16):
            if (j, k0) in copies:
                copies[j, k0].wait()
            x = held[j, :some, k0 : min(k0 + 16, noff), :]
            if k0 + 16 > noff:
                x = jnp.concatenate([x.astype(F32), jnp.zeros((some, k0 + 16 - noff, terms), F32)], axis=1).astype(BF)
            if some < 16:
                x = jnp.concatenate([x, jnp.zeros((16 - some, 16, terms), BF)], axis=0)
            x = jnp.concatenate([x, jnp.zeros((16, 16, LANES - terms), BF)], axis=2)
            out_ref[k0 : k0 + 16, rows, :] = jnp.swapaxes(x, 0, 1)


def by_operator(ops, first, steps):
    noff, terms, _ = ops.shape
    total = up(noff, 16)
    return pl.pallas_call(
        functools.partial(by_operator_kernel, first),
        in_specs=[pl.BlockSpec(memory_space=pl.ANY)],
        out_specs=pl.BlockSpec(memory_space=pltpu.VMEM),
        out_shape=pltpu.VMEM((total, steps * 16, LANES), BF),
        scratch_shapes=[pltpu.VMEM((steps, 16, noff, terms), BF), pltpu.SemaphoreType.DMA((steps + 3,))],
        compiler_params=pltpu.CompilerParams(vmem_limit_bytes=16 * 2**20),
        cost_estimate=pl.CostEstimate(flops=0, bytes_accessed=2 * total * steps * 16 * LANES * 2, transcendentals=0),
        name="by_operator",
    )(pltpu.with_memory_space_constraint(jnp.transpose(ops, (1, 0, 2)), pltpu.HBM))


INNER = [(3, None), (4, None), (5, None), (2, 1), (6, 0)]
OUTER = [(1, None), (2, None), (6, None), (7, None), (0, 1), (8, 0)]


def shift_sources(pairs, grid, out_ref):
    parity = lax.broadcasted_iota(jnp.int32, (BZ, LANES), 0) % 2
    nothing = jnp.zeros((BZ, LANES), F32)
    for dz in range(-REACH, REACH + 1):
        for x in range(EXT):
            turned = {}

            def tile(y):
                if y not in turned:
                    t = grid[x, y]
                    if dz:
                        t = pltpu.roll(t, (-dz) % BZ, 0)
                    if abs(dz) == REACH:
                        t = jnp.where(parity == (0 if dz > 0 else 1), t, 0.0)
                    turned[y] = t
                return turned[y]

            for n, (y, keep) in enumerate(pairs):
                halves = [tile(y + i) if keep in (None, i) else nothing for i in range(2)]
                out_ref[((dz + REACH) * len(pairs) + n) * EXT + x] = jnp.concatenate(halves, axis=0).astype(BF)


def shifted_sources(inner, outer, offset):
    dx, dy, dz = offset
    tiles = []
    for bx in range(BX):
        for h in range(2):
            pair = (dy + REACH + 2 * h, {-REACH: 1, REACH: 0}.get(dy))
            ref, pairs = (inner, INNER) if pair in INNER else (outer, OUTER)
            if abs(dx) == REACH and bx % 2 != (0 if dx > 0 else 1):
                tiles.append(jnp.zeros((16, LANES), BF))
            else:
                tiles.append(ref[((dz + REACH) * len(pairs) + pairs.index(pair)) * EXT + REACH + dx + bx])
    return jnp.concatenate(tiles, axis=0)


def one_hot(index, rows):
    at = lax.broadcasted_iota(jnp.int32, (rows, index.shape[1]), 0)
    return (at == index).astype(F32).astype(BF)


def split3(x):
    high = x.astype(BF).astype(F32)
    middle = (x - high).astype(BF).astype(F32)
    return jnp.concatenate([high, middle, x - high - middle], axis=0).astype(BF)


def nt(a, b):
    return lax.dot_general(a, b, (((1,), (1,)), ((), ())), preferred_element_type=F32)


def neighbours(size_x, size_y):
    ix, iy = lax.axis_index("xs"), lax.axis_index("ys")
    step_x = [0, 1 - 2 * lax.rem(ix, 2), 2 * lax.rem(ix, 2) - 1]
    step_y = [0, 1 - 2 * lax.rem(iy, 2), 2 * lax.rem(iy, 2) - 1]
    return [
        lax.rem(ix + step_x[x] + size_x, size_x) * size_y + lax.rem(iy + step_y[y] + size_y, size_y)
        for x, y in AROUND
    ]


def pack_kernel(sizes, owner_hbm, slot_hbm, table_hbm, multipoles_hbm, evaluation_ref, ion_hbm,
                own_ref, x_even_ref, x_odd_ref, y_even_ref, y_odd_ref, rows_ref, place_ref,
                held, owner_ref, slot_ref, table_ref, multipoles_ref, ion_ref, sems):
    terms = multipoles_ref.shape[0]
    groups = held.shape[0]
    above = offsets().index((0, 0, 2))
    small = [(table_hbm.at[above // 8 * 8 : above // 8 * 8 + 8, :], table_ref), (multipoles_hbm, multipoles_ref),
             (owner_hbm, owner_ref), (slot_hbm, slot_ref), (ion_hbm, ion_ref)]
    copies = [pltpu.make_async_copy(evaluation_ref.at[:, 16 * j : 16 * j + 16, :], held.at[j], sems.at[j])
              for j in range(groups)]
    copies += [pltpu.make_async_copy(a, b, sems.at[groups + i]) for i, (a, b) in enumerate(small)]
    for copy in copies[groups:] + copies[:groups]:
        copy.start()
    for copy in copies[groups:]:
        copy.wait()
    chunks = slot_ref.shape[0]
    per_peer = place_ref.shape[0] // 8
    row = table_ref[above % 8 : above % 8 + 1, :]
    z = lax.broadcasted_iota(jnp.int32, row.shape, 1) % BZ
    row = jnp.where(z >= 2, pltpu.roll(row, 2, 1), pltpu.roll(row, LANES - 6, 1))
    masked = jnp.where(row >= 0, multipoles_ref[...].astype(F32), 0.0)
    masked = jnp.concatenate([masked, jnp.zeros((LANES - terms, LANES), F32)], axis=0).T
    own_ref[...] = masked.astype(BF)
    even_x = lax.rem(lax.axis_index("xs"), 2) == 0
    lower, upper = masked[:SLAB_X], masked[LANES - SLAB_X :]
    x_even_ref[:SLAB_X] = jnp.where(even_x, upper, lower).astype(BF)
    x_odd_ref[:SLAB_X] = jnp.where(even_x, lower, upper).astype(BF)

    owner = owner_ref[...]
    member = [(owner == device).astype(F32) for device in neighbours(*sizes)]
    stacked = jnp.concatenate(member, axis=0).astype(BF)
    n = 8 * chunks
    r = lax.broadcasted_iota(jnp.int32, (n, n), 0)
    c = lax.broadcasted_iota(jnp.int32, (n, n), 1)
    earlier = ((r // chunks == c // chunks) & (c < r)).astype(F32).astype(BF)
    r = lax.broadcasted_iota(jnp.int32, (LANES, LANES), 0)
    c = lax.broadcasted_iota(jnp.int32, (LANES, LANES), 1)
    before = (r < c).astype(F32).astype(BF)
    ones = jnp.ones((LANES, LANES), BF)
    ahead = jnp.dot(earlier, stacked, preferred_element_type=F32).astype(BF)
    rank = jnp.dot(stacked, before, preferred_element_type=F32) + jnp.dot(ahead, ones, preferred_element_type=F32)
    place = jnp.full((chunks, LANES), -1.0, F32)
    for d in range(8):
        place = jnp.where(member[d] > 0, rank[d * chunks : (d + 1) * chunks] + d * per_peer, place)
    place = place.astype(jnp.int32)
    for j in range(chunks):
        place_ref[:, j * LANES : (j + 1) * LANES] = one_hot(place[j : j + 1], 8 * per_peer)

    half_way = groups // 2 * 4 * LANES

    def picked_by(first, last):
        x = rows_ref[:, :, first:last].reshape(FIELDS * LANES, last - first)
        return nt(x, place_ref[:, first:last])

    slot = slot_ref[...].astype(F32)
    for j in range(chunks // 4):
        part = slice(16 * j, 16 * j + 16)
        if j == groups // 2:
            picked = picked_by(0, half_way)
        slots = [jnp.broadcast_to(slot[4 * j + i : 4 * j + i + 1], (4, LANES)) for i in range(4)]
        extra = [ion_ref[part, :], jnp.concatenate(slots, axis=0).astype(BF)]
        extra = jnp.concatenate([e.reshape(1, 16, LANES) for e in extra], axis=0)
        copies[j].wait()
        for p in range(0, LANES, 16):
            x = held[j, p : min(p + 16, terms)]
            if p + 16 > terms:
                x = jnp.concatenate([x, extra, jnp.zeros((16 - x.shape[0] - 2, 16, LANES), BF)], axis=0)
            x = jnp.swapaxes(x, 0, 1)
            for i in range(4):
                lanes = slice((4 * j + i) * LANES, (4 * j + i + 1) * LANES)
                for f in range(FIELDS):
                    rows_ref[f, p : p + 16, lanes] = x[4 * i + f]

    picked = picked + picked_by(half_way, place_ref.shape[1])

    targets = {
        (1, 1): (x_even_ref, 0), (1, 0): (x_even_ref, 1), (1, 2): (x_even_ref, 2),
        (2, 1): (x_odd_ref, 0), (2, 0): (x_odd_ref, 1), (2, 2): (x_odd_ref, 2),
        (0, 1): (y_even_ref, 0), (0, 2): (y_odd_ref, 0),
    }
    lane = lax.broadcasted_iota(jnp.int32, (LANES, LANES), 1) // per_peer
    each = LANES // per_peer
    turned = []
    for half in range(2):
        x = [picked[f * LANES : (f + 1) * LANES, half * LANES : (half + 1) * LANES] for f in range(FIELDS)]
        turned.append([pltpu.roll(t, f * per_peer, 1) if f else t for f, t in enumerate(x)])
    for d, where in enumerate(AROUND):
        message = turned[d // each][0]
        for f in range(1, FIELDS):
            message = jnp.where(lane == (f + d) % each, turned[d // each][f], message)
        ref, at = targets[where]
        at = at * LANES + (SLAB_X if where[0] else 0)
        ref[at : at + LANES] = message.astype(BF)


def pack(sizes, owner, slot, table, multipoles, evaluation, ions):
    terms = multipoles.shape[0]
    atoms = slot.shape[0]
    chunks = atoms // LANES
    per_peer = atoms // 64
    whole = pl.BlockSpec(memory_space=pltpu.VMEM)
    view = evaluation.transpose(1, 0, 2).reshape(terms, FIELDS, chunks, LANES)
    view = view.transpose(0, 2, 1, 3).reshape(terms, FIELDS * chunks, LANES)
    ions = ions.reshape(FIELDS, chunks, LANES).transpose(1, 0, 2).reshape(FIELDS * chunks, LANES)
    block = lambda rows: jax.ShapeDtypeStruct((rows, LANES), BF)
    return pl.pallas_call(
        functools.partial(pack_kernel, sizes),
        in_specs=[pl.BlockSpec(memory_space=pl.ANY)] * 6,
        out_specs=[whole] * 7,
        out_shape=[block(LANES), block(SLAB_X + 3 * LANES), block(SLAB_X + 3 * LANES), block(LANES), block(LANES),
                   pltpu.VMEM((FIELDS, LANES, atoms), BF),
                   pltpu.VMEM((8 * per_peer, atoms), BF)],
        scratch_shapes=[
            pltpu.VMEM((chunks // 4, terms, 16, LANES), BF),
            pltpu.VMEM((chunks, LANES), jnp.int32),
            pltpu.VMEM((chunks, LANES), jnp.int32),
            pltpu.VMEM((8, LANES), jnp.int32),
            pltpu.VMEM((terms, LANES), BF),
            pltpu.VMEM((FIELDS * chunks, LANES), BF),
            pltpu.SemaphoreType.DMA((chunks // 4 + 5,)),
        ],
        compiler_params=pltpu.CompilerParams(vmem_limit_bytes=24 * 2**20),
        name="pack",
    )(*(pltpu.with_memory_space_constraint(x, pltpu.HBM) for x in (
        owner.reshape(chunks, LANES), slot.reshape(chunks, LANES), table, multipoles, view, ions)))


def tiles_of(ref, first, shape):
    nx, ny = shape
    value = ref[first : first + nx * ny * BZ, :].astype(F32)
    return {(x, y): value[(x * ny + y) * BZ : (x * ny + y + 1) * BZ] for x in range(nx) for y in range(ny)}


def forward_kernel(own, x_even, x_odd, y_even_message, y_odd_message, y_even_ref, y_odd_ref, odd_messages_ref):
    even_y = lax.rem(lax.axis_index("ys"), 2) == 0
    lower, upper = [], []
    for ref, nx in ((own, BX), (x_even, REACH), (x_odd, REACH)):
        tiles = tiles_of(ref, 0, (nx, BY))
        lower += [tiles[x, y] for x in range(nx) for y in range(REACH)]
        upper += [tiles[x, y + BY - REACH] for x in range(nx) for y in range(REACH)]
    lower, upper = jnp.concatenate(lower, axis=0), jnp.concatenate(upper, axis=0)
    y_even_ref[:SLAB_Y] = jnp.where(even_y, upper, lower).astype(BF)
    y_odd_ref[:SLAB_Y] = jnp.where(even_y, lower, upper).astype(BF)
    y_even_ref[SLAB_Y : SLAB_Y + LANES] = y_even_message[...]
    y_odd_ref[SLAB_Y:] = y_odd_message[...]
    for ref, to, at in ((y_even_ref, SLAB_Y + LANES, 0), (odd_messages_ref, 0, 2)):
        for i, source in enumerate((x_even, x_odd)):
            first = SLAB_X + at * LANES
            ref[to + i * LANES : to + (i + 1) * LANES] = source[first : first + LANES]


def forward(*operands):
    vmem = pl.BlockSpec(memory_space=pltpu.VMEM)
    return pl.pallas_call(
        forward_kernel,
        in_specs=[vmem] * 5,
        out_specs=[vmem] * 3,
        out_shape=[pltpu.VMEM((rows, LANES), BF) for rows in (SLAB_Y + 3 * LANES, SLAB_Y + LANES, 2 * LANES)],
        compiler_params=pltpu.CompilerParams(vmem_limit_bytes=4 * 2**20),
        name="forward",
    )(*operands)


def sources_along_x(own, x_even, x_odd):
    even_x = lax.rem(lax.axis_index("xs"), 2) == 0
    found = {(REACH + x, REACH + y): t for (x, y), t in tiles_of(own, 0, (BX, BY)).items()}
    a, b = tiles_of(x_even, 0, (REACH, BY)), tiles_of(x_odd, 0, (REACH, BY))
    for x, y in a:
        found[x, REACH + y] = jnp.where(even_x, b[x, y], a[x, y])
        found[REACH + BX + x, REACH + y] = jnp.where(even_x, a[x, y], b[x, y])
    return found


def sources_along_y(y_even, y_odd):
    even_x = lax.rem(lax.axis_index("xs"), 2) == 0
    even_y = lax.rem(lax.axis_index("ys"), 2) == 0
    strips = []
    for ref in (y_even, y_odd):
        strip = {(REACH + x, y): t for (x, y), t in tiles_of(ref, 0, (BX, REACH)).items()}
        first = BX * REACH * BZ
        a = tiles_of(ref, first, (REACH, REACH))
        b = tiles_of(ref, first + REACH * REACH * BZ, (REACH, REACH))
        for x, y in a:
            strip[x, y] = jnp.where(even_x, b[x, y], a[x, y])
            strip[REACH + BX + x, y] = jnp.where(even_x, a[x, y], b[x, y])
        strips.append(strip)
    found = {}
    for x, y in strips[0]:
        found[x, y] = jnp.where(even_y, strips[1][x, y], strips[0][x, y])
        found[x, REACH + BY + y] = jnp.where(even_y, strips[0][x, y], strips[1][x, y])
    return found


def inner_kernel(own, x_even, x_odd, shifted_ref, grid_ref):
    for (x, y), box in sources_along_x(own, x_even, x_odd).items():
        grid_ref[x, y] = box
    shift_sources(INNER, grid_ref, shifted_ref)


def inner_pairs(own, x_even, x_odd):
    vmem = pl.BlockSpec(memory_space=pltpu.VMEM)
    return pl.pallas_call(
        inner_kernel,
        in_specs=[vmem] * 3,
        out_specs=[vmem] * 2,
        out_shape=[pltpu.VMEM((NSHIFT * len(INNER) * EXT, 16, LANES), BF), pltpu.VMEM((EXT, REACH + BY, BZ, LANES), F32)],
        compiler_params=pltpu.CompilerParams(vmem_limit_bytes=8 * 2**20),
        cost_estimate=pl.CostEstimate(flops=0, bytes_accessed=3 * 2**20, transcendentals=0),
        name="inner_pairs",
    )(own, x_even, x_odd)


def messages(x_even, x_odd, y_even, y_odd, odd_passed):
    direct = SLAB_X + LANES
    return [
        (x_even, direct), (y_even, SLAB_Y + LANES), (odd_passed, 0),
        (x_odd, direct), (y_even, SLAB_Y + 2 * LANES), (odd_passed, LANES),
        (y_even, SLAB_Y), (y_odd, SLAB_Y),
    ]


def m2l_kernel(inner, along_x, y_odd, y_even, first_ref, second_ref, local_ref, grid, outer):
    for (x, y), box in sources_along_y(y_even, y_odd).items():
        grid[x, y] = box
    for x in range(EXT):
        for y in (REACH, REACH + BY - 1):
            grid[x, y] = along_x[x, y]
    shift_sources(OUTER, grid, outer)
    listed = offsets()
    acc = jnp.zeros((LANES, LANES), F32)
    for k0 in range(0, len(listed), STEP):
        some = range(k0, min(k0 + STEP, len(listed)))
        a = [jnp.concatenate([first_ref[k], second_ref[k]], axis=0) for k in some]
        b = [shifted_sources(inner, outer, listed[k]) for k in some]
        acc = acc + nt(jnp.concatenate(a, axis=1), jnp.concatenate(b, axis=1))
    local_ref[...] = acc.astype(BF)


def m2l(inner, along_x, y_odd, y_even, first, second):
    vmem = pl.BlockSpec(memory_space=pltpu.VMEM)
    pinned = [pltpu.with_memory_space_constraint(x, pltpu.VMEM) for x in (inner, along_x, first, second)]
    return pl.pallas_call(
        m2l_kernel,
        in_specs=[vmem] * 6,
        out_specs=vmem,
        out_shape=jax.ShapeDtypeStruct((LANES, LANES), BF),
        scratch_shapes=[
            pltpu.VMEM((EXT, EXT, BZ, LANES), F32),
            pltpu.VMEM((NSHIFT * len(OUTER) * EXT, 16, LANES), BF),
        ],
        compiler_params=pltpu.CompilerParams(vmem_limit_bytes=16 * 2**20),
        cost_estimate=pl.CostEstimate(flops=0, bytes_accessed=2**16, transcendentals=0),
        name="m2l",
    )(pinned[0], pinned[1], y_odd, y_even, pinned[2], pinned[3])


def answer_kernel(terms, local_ref, x_odd, x_even, y_odd, y_even, odd_passed, by_even_ref, by_odd_ref, by_y_ref, tail_ref):
    local = local_ref[...]
    row = lax.broadcasted_iota(jnp.int32, (8, LANES), 0)
    answers = []
    for i, (ref, at) in enumerate(messages(x_even, x_odd, y_even, y_odd, odd_passed)):
        x = ref[at : at + LANES, :].astype(F32)
        tail_ref[i : i + 1] = x[terms : terms + 1]
        tail_ref[8 + i : 9 + i] = x[terms + 1 : terms + 2]
        spread = one_hot(x[terms + 1 : terms + 2].astype(jnp.int32), LANES)
        column = jnp.dot(local, spread, preferred_element_type=F32)
        answers.append(jnp.sum(x[:terms] * column[:terms], axis=0, keepdims=True))
    for ref, first in ((by_even_ref, 0), (by_odd_ref, 3), (by_y_ref, 6)):
        tile = jnp.zeros((8, LANES), F32)
        for i in range(min(3, 8 - first)):
            tile = jnp.where(row == i, answers[first + i], tile)
        ref[...] = tile


def answer(terms, *operands):
    vmem = pl.BlockSpec(memory_space=pltpu.VMEM)
    return pl.pallas_call(
        functools.partial(answer_kernel, terms),
        in_specs=[vmem] * 6,
        out_specs=[vmem] * 4,
        out_shape=[jax.ShapeDtypeStruct((8, LANES), F32)] * 3 + [jax.ShapeDtypeStruct((16, LANES), F32)],
        compiler_params=pltpu.CompilerParams(vmem_limit_bytes=4 * 2**20),
        name="answer",
    )(*operands)


def atoms_kernel(size_y, owner_ref, slot_ref, ion_ref, rows_ref, local_ref, tail_ref,
                 by_even_ref, by_odd_ref, by_y_ref, local_exp_ref, far_ref, virial_ref):
    chunks = slot_ref.shape[0]
    local = local_ref[...]
    local_exp_ref[...] = local[: local_exp_ref.shape[0]]
    slots = jnp.where(owner_ref[...] == lax.axis_index("xs") * size_y + lax.axis_index("ys"), slot_ref[...], -1)
    row = lax.broadcasted_iota(jnp.int32, (8, LANES), 0)
    total = jnp.zeros((9 * 8, LANES), F32)
    for j in range(chunks):
        lanes = slice(j * LANES, (j + 1) * LANES)
        spread = one_hot(slots[j : j + 1], LANES)
        column = jnp.dot(local, spread, preferred_element_type=F32)
        far = jnp.zeros((8, LANES), F32)
        for f in range(FIELDS):
            value = jnp.sum(rows_ref[f, :, lanes].astype(F32) * column, axis=0, keepdims=True)
            far = jnp.where(row == f, value, far)
        far_ref[:, lanes] = far[:FIELDS]
        ion = ion_ref[j * FIELDS : (j + 1) * FIELDS, :].astype(F32)
        terms3 = jnp.concatenate([ion[0:1] * ion[a : a + 1] * far for a in (1, 2, 3)], axis=0)
        total = total + nt(split3(terms3), spread)

    per_peer = by_y_ref.shape[1] // FIELDS
    group = lax.broadcasted_iota(jnp.int32, (8, LANES), 1) // per_peer
    answers = [(ref, i) for ref in (by_even_ref, by_odd_ref) for i in range(3)] + [(by_y_ref, 0), (by_y_ref, 1)]
    for n, (answer, i) in enumerate(answers):
        d = AROUND.index(SENDERS[n])
        spread = one_hot(tail_ref[8 + n : 9 + n].astype(jnp.int32), LANES)
        ion = jnp.broadcast_to(tail_ref[n : n + 1], (8, LANES))

        def everywhere(f):
            x = jnp.where(group == (f + d) % FIELDS, ion, 0.0)
            x = x + pltpu.roll(x, 2 * per_peer, 1)
            return x + pltpu.roll(x, per_peer, 1)

        far = jnp.where(group == (row + d) % FIELDS, jnp.broadcast_to(answer[i : i + 1, :], (8, LANES)), 0.0)
        charge = everywhere(0)
        terms3 = jnp.concatenate([charge * everywhere(a) * far for a in (1, 2, 3)], axis=0)
        total = total + nt(split3(terms3), spread)
    virial = total[:24] + total[24:48] + total[48:]
    for a in range(3):
        virial_ref[3 * a : 3 * a + 3, :] = virial[8 * a + 1 : 8 * a + 4]


def atoms_of_device(terms, size_y, owner, slot, ions, rows, local, tail, down, up_, side):
    atoms = slot.shape[0]
    chunks = atoms // LANES
    whole = pl.BlockSpec(memory_space=pltpu.VMEM)
    ions = ions.reshape(FIELDS, chunks, LANES).transpose(1, 0, 2).reshape(FIELDS * chunks, LANES)
    return pl.pallas_call(
        functools.partial(atoms_kernel, size_y),
        in_specs=[whole] * 9,
        out_specs=[whole] * 3,
        out_shape=[jax.ShapeDtypeStruct((terms, LANES), BF), jax.ShapeDtypeStruct((FIELDS, atoms), F32),
                   jax.ShapeDtypeStruct((9, LANES), F32)],
        compiler_params=pltpu.CompilerParams(vmem_limit_bytes=16 * 2**20),
        cost_estimate=pl.CostEstimate(flops=4 * 10**6, bytes_accessed=8 * 2**20, transcendentals=0),
        name="atoms",
    )(owner.reshape(chunks, LANES), slot.reshape(chunks, LANES), ions, pltpu.with_memory_space_constraint(rows, pltpu.VMEM), local, tail, down, up_, side)


def turn_kernel(answer_y, x_even, x_odd, y_odd_ref, y_even_ref):
    for n, ref in ((1, y_even_ref), (2, y_odd_ref)):
        ref[...] = jnp.zeros(ref.shape, F32)
        ref[0:1] = answer_y[n - 1 : n]
        ref[1:2] = x_even[n : n + 1]
        ref[2:3] = x_odd[n : n + 1]


def turn(*operands):
    vmem = pl.BlockSpec(memory_space=pltpu.VMEM)
    return pl.pallas_call(
        turn_kernel,
        in_specs=[vmem] * 3,
        out_specs=[vmem] * 2,
        out_shape=[jax.ShapeDtypeStruct((8, LANES), F32)] * 2,
        compiler_params=pltpu.CompilerParams(vmem_limit_bytes=2**20),
        name="turn",
    )(*operands)


def merge_kernel(far_ref, place_ref, x_odd, x_even, y_odd, y_even, out_ref):
    per_peer = place_ref.shape[0] // 8
    each = LANES // per_peer
    returned = {
        (1, 0): (x_even, 0), (2, 0): (x_odd, 0),
        (0, 1): (y_even, 0), (1, 1): (y_even, 1), (2, 1): (y_even, 2),
        (0, 2): (y_odd, 0), (1, 2): (y_odd, 1), (2, 2): (y_odd, 2),
    }
    row = lax.broadcasted_iota(jnp.int32, (8, LANES), 0)
    group = lax.broadcasted_iota(jnp.int32, (8, LANES), 1) // per_peer
    halves = []
    for half in range(2):
        x = []
        for where in AROUND[half * each : half * each + each]:
            ref, i = returned[where]
            x.append(jnp.broadcast_to(ref[i : i + 1, :], (8, LANES)))
        tile = jnp.zeros((8, LANES), F32)
        for f in range(FIELDS):
            y = x[0]
            for g in range(1, each):
                y = jnp.where(group == (f + g) % each, x[g], y)
            tile = jnp.where(row == f, pltpu.roll(y, (each - f) * per_peer, 1) if f else y, tile)
        halves.append(tile)
    back = split3(jnp.concatenate(halves, axis=1))
    added = jnp.dot(back, place_ref[...], preferred_element_type=F32)
    out_ref[...] = far_ref[...] + (added[:FIELDS] + added[8 : 8 + FIELDS] + added[16 : 16 + FIELDS])


def merge(far, place, *returned):
    whole = pl.BlockSpec(memory_space=pltpu.VMEM)
    return pl.pallas_call(
        merge_kernel,
        in_specs=[whole] * 6,
        out_specs=whole,
        out_shape=jax.ShapeDtypeStruct(far.shape, F32),
        compiler_params=pltpu.CompilerParams(vmem_limit_bytes=16 * 2**20),
        name="merge",
    )(far, pltpu.with_memory_space_constraint(place, pltpu.VMEM), *returned)


def across(axis, edge, block):
    count = lax.axis_size(axis)
    pairs = [(i, (i + 1) % count) for i in range(edge - 1, count, 2)]
    return lax.ppermute(block, axis, pairs + [(b, a) for a, b in pairs])


def shards(
    multipoles,
    translation_ops,
    target_interaction_table,
    evaluation,
    ion_data,
    atom_owner,
    atom_slot,
):
    num_terms = multipoles.shape[0]
    size_x = lax.axis_size("xs")
    size_y = lax.axis_size("ys")
    own, to_x_even, to_x_odd, y_even_message, y_odd_message, rows, place = pack(
        (size_x, size_y), atom_owner, atom_slot, target_interaction_table, multipoles, evaluation, ion_data
    )
    x_even = across("xs", 1, to_x_even)
    x_odd = across("xs", 2, to_x_odd)
    first = by_operator(translation_ops, 0, 5)
    x_even, x_odd, first = lax.optimization_barrier((x_even, x_odd, first))
    to_y_even, to_y_odd, odd_messages = forward(own, x_even, x_odd, y_even_message, y_odd_message)
    y_odd = across("ys", 2, to_y_odd)
    y_even = across("ys", 1, to_y_even)
    odd_messages = across("ys", 2, odd_messages)
    second = by_operator(translation_ops, 5, 3)
    inner, along_x = inner_pairs(own, x_even, x_odd)
    local = m2l(inner, along_x, y_odd, y_even, first, second)
    answer_x_even, answer_x_odd, answer_y, tail = answer(
        num_terms, local, x_odd, x_even, y_odd, y_even, odd_messages
    )

    back_x_even = across("xs", 1, answer_x_even)
    back_x_odd = across("xs", 2, answer_x_odd)
    local_exp, far, box_virial = atoms_of_device(
        num_terms, size_y, atom_owner, atom_slot, ion_data, rows, local, tail, answer_x_even, answer_x_odd, answer_y
    )
    back_x_even, back_x_odd, far = lax.optimization_barrier((back_x_even, back_x_odd, far))
    answer_y_odd, answer_y_even = turn(answer_y, back_x_even, back_x_odd)
    back_y_odd = across("ys", 2, answer_y_odd)
    back_y_even = across("ys", 1, answer_y_even)
    atom_far_field = merge(far, place, back_x_odd, back_x_even, back_y_odd, back_y_even)
    return (local_exp, atom_far_field, box_virial)


def solution(mesh):
    placed = (
        P(None, ("xs", "ys")),
        P(),
        P(None, ("xs", "ys")),
        P(None, None, ("xs", "ys")),
        P(None, ("xs", "ys")),
        P(("xs", "ys"), None),
        P(("xs", "ys")),
    )
    return jax.shard_map(
        shards,
        mesh=mesh,
        in_specs=placed,
        out_specs=(P(None, ("xs", "ys")), P(None, ("xs", "ys")), P(None, ("xs", "ys"))),
        check_vma=False,
    )
```

```python
import functools

import jax
import jax.numpy as jnp
from jax import lax
from jax.experimental import pallas as pl
from jax.experimental.pallas import tpu as pltpu
from jax.sharding import PartitionSpec as P

BF = jnp.bfloat16
F32 = jnp.float32
REACH = 3
NSHIFT = 2 * REACH + 1
LANES = 128
BX = 4
BY = 4
BZ = 8
EXT = BX + 2 * REACH
SLAB_X = REACH * BY * BZ
SLAB_Y = BX * REACH * BZ + 2 * REACH * REACH * BZ
FIELDS = 4
STEP = 40
AROUND = [(1, 1), (1, 0), (1, 2), (2, 1), (2, 0), (2, 2), (0, 1), (0, 2)]
SENDERS = [(1, 0), (1, 1), (1, 2), (2, 0), (2, 1), (2, 2), (0, 1), (0, 2)]


def offsets():
    listed = []
    for dx in range(-REACH, REACH + 1):
        for dy in range(-REACH, REACH + 1):
            for dz in range(-REACH, REACH + 1):
                if max(abs(dx), abs(dy), abs(dz)) >= 2:
                    listed.append((dx, dy, dz))
    return listed


def up(value, unit):
    return -(-value // unit) * unit


def by_operator_kernel(first, ops_ref, out_ref, held, sems):
    terms, noff, _ = ops_ref.shape
    total = out_ref.shape[0]
    part = up(total // 4, 16)
    cuts = [slice(k, min(k + part, noff)) for k in range(0, noff, part)]
    copies = {}
    for j in range(held.shape[0]):
        q = (first + j) * 16
        some = min(16, terms - q)
        for n, cut in enumerate(cuts if j == 0 else [slice(0, noff)]):
            copies[j, cut.start] = pltpu.make_async_copy(
                ops_ref.at[q : q + some, cut, :], held.at[j, :some, cut, :], sems.at[n if j == 0 else j + len(cuts) - 1]
            )
            copies[j, cut.start].start()
    for j in range(held.shape[0]):
        some = min(16, terms - (first + j) * 16)
        rows = slice(16 * j, 16 * j + 16)
        for k0 in range(0, total, 16):
            if (j, k0) in copies:
                copies[j, k0].wait()
            x = held[j, :some, k0 : min(k0 + 16, noff), :]
            if k0 + 16 > noff:
                x = jnp.concatenate([x.astype(F32), jnp.zeros((some, k0 + 16 - noff, terms), F32)], axis=1).astype(BF)
            if some < 16:
                x = jnp.concatenate([x, jnp.zeros((16 - some, 16, terms), BF)], axis=0)
            x = jnp.concatenate([x, jnp.zeros((16, 16, LANES - terms), BF)], axis=2)
            out_ref[k0 : k0 + 16, rows, :] = jnp.swapaxes(x, 0, 1)


def by_operator(ops, first, steps):
    noff, terms, _ = ops.shape
    total = up(noff, 16)
    return pl.pallas_call(
        functools.partial(by_operator_kernel, first),
        in_specs=[pl.BlockSpec(memory_space=pl.ANY)],
        out_specs=pl.BlockSpec(memory_space=pltpu.VMEM),
        out_shape=pltpu.VMEM((total, steps * 16, LANES), BF),
        scratch_shapes=[pltpu.VMEM((steps, 16, noff, terms), BF), pltpu.SemaphoreType.DMA((steps + 3,))],
        compiler_params=pltpu.CompilerParams(vmem_limit_bytes=16 * 2**20),
        cost_estimate=pl.CostEstimate(flops=0, bytes_accessed=2 * total * steps * 16 * LANES * 2, transcendentals=0),
        name="by_operator",
    )(pltpu.with_memory_space_constraint(jnp.transpose(ops, (1, 0, 2)), pltpu.HBM))


INNER = [(3, None), (4, None), (5, None), (2, 1), (6, 0)]
OUTER = [(1, None), (2, None), (6, None), (7, None), (0, 1), (8, 0)]


def shift_sources(pairs, grid, out_ref):
    parity = lax.broadcasted_iota(jnp.int32, (BZ, LANES), 0) % 2
    nothing = jnp.zeros((BZ, LANES), F32)
    for dz in range(-REACH, REACH + 1):
        for x in range(EXT):
            turned = {}

            def tile(y):
                if y not in turned:
                    t = grid[x, y]
                    if dz:
                        t = pltpu.roll(t, (-dz) % BZ, 0)
                    if abs(dz) == REACH:
                        t = jnp.where(parity == (0 if dz > 0 else 1), t, 0.0)
                    turned[y] = t
                return turned[y]

            for n, (y, keep) in enumerate(pairs):
                halves = [tile(y + i) if keep in (None, i) else nothing for i in range(2)]
                out_ref[((dz + REACH) * len(pairs) + n) * EXT + x] = jnp.concatenate(halves, axis=0).astype(BF)


def shifted_sources(inner, outer, offset):
    dx, dy, dz = offset
    tiles = []
    for bx in range(BX):
        for h in range(2):
            pair = (dy + REACH + 2 * h, {-REACH: 1, REACH: 0}.get(dy))
            ref, pairs = (inner, INNER) if pair in INNER else (outer, OUTER)
            if abs(dx) == REACH and bx % 2 != (0 if dx > 0 else 1):
                tiles.append(jnp.zeros((16, LANES), BF))
            else:
                tiles.append(ref[((dz + REACH) * len(pairs) + pairs.index(pair)) * EXT + REACH + dx + bx])
    return jnp.concatenate(tiles, axis=0)


def one_hot(index, rows):
    at = lax.broadcasted_iota(jnp.int32, (rows, index.shape[1]), 0)
    return (at == index).astype(F32).astype(BF)


def split3(x):
    high = x.astype(BF).astype(F32)
    middle = (x - high).astype(BF).astype(F32)
    return jnp.concatenate([high, middle, x - high - middle], axis=0).astype(BF)


def nt(a, b):
    return lax.dot_general(a, b, (((1,), (1,)), ((), ())), preferred_element_type=F32)


def neighbours(size_x, size_y):
    ix, iy = lax.axis_index("xs"), lax.axis_index("ys")
    step_x = [0, 1 - 2 * lax.rem(ix, 2), 2 * lax.rem(ix, 2) - 1]
    step_y = [0, 1 - 2 * lax.rem(iy, 2), 2 * lax.rem(iy, 2) - 1]
    return [
        lax.rem(ix + step_x[x] + size_x, size_x) * size_y + lax.rem(iy + step_y[y] + size_y, size_y)
        for x, y in AROUND
    ]


def pack_kernel(sizes, owner_hbm, slot_hbm, table_hbm, multipoles_hbm, evaluation_ref, ion_hbm,
                own_ref, x_even_ref, x_odd_ref, y_even_ref, y_odd_ref, rows_ref, place_ref,
                held, owner_ref, slot_ref, table_ref, multipoles_ref, ion_ref, sems):
    terms = multipoles_ref.shape[0]
    groups = held.shape[0]
    above = offsets().index((0, 0, 2))
    small = [(table_hbm.at[above // 8 * 8 : above // 8 * 8 + 8, :], table_ref), (multipoles_hbm, multipoles_ref),
             (owner_hbm, owner_ref), (slot_hbm, slot_ref), (ion_hbm, ion_ref)]
    copies = [pltpu.make_async_copy(evaluation_ref.at[:, 16 * j : 16 * j + 16, :], held.at[j], sems.at[j])
              for j in range(groups)]
    copies += [pltpu.make_async_copy(a, b, sems.at[groups + i]) for i, (a, b) in enumerate(small)]
    for copy in copies[groups:] + copies[:groups]:
        copy.start()
    for copy in copies[groups:]:
        copy.wait()
    chunks = slot_ref.shape[0]
    per_peer = place_ref.shape[0] // 8
    row = table_ref[above % 8 : above % 8 + 1, :]
    z = lax.broadcasted_iota(jnp.int32, row.shape, 1) % BZ
    row = jnp.where(z >= 2, pltpu.roll(row, 2, 1), pltpu.roll(row, LANES - 6, 1))
    masked = jnp.where(row >= 0, multipoles_ref[...].astype(F32), 0.0)
    masked = jnp.concatenate([masked, jnp.zeros((LANES - terms, LANES), F32)], axis=0).T
    own_ref[...] = masked.astype(BF)
    even_x = lax.rem(lax.axis_index("xs"), 2) == 0
    lower, upper = masked[:SLAB_X], masked[LANES - SLAB_X :]
    x_even_ref[:SLAB_X] = jnp.where(even_x, upper, lower).astype(BF)
    x_odd_ref[:SLAB_X] = jnp.where(even_x, lower, upper).astype(BF)

    owner = owner_ref[...]
    member = [(owner == device).astype(F32) for device in neighbours(*sizes)]
    stacked = jnp.concatenate(member, axis=0).astype(BF)
    n = 8 * chunks
    r = lax.broadcasted_iota(jnp.int32, (n, n), 0)
    c = lax.broadcasted_iota(jnp.int32, (n, n), 1)
    earlier = ((r // chunks == c // chunks) & (c < r)).astype(F32).astype(BF)
    r = lax.broadcasted_iota(jnp.int32, (LANES, LANES), 0)
    c = lax.broadcasted_iota(jnp.int32, (LANES, LANES), 1)
    before = (r < c).astype(F32).astype(BF)
    ones = jnp.ones((LANES, LANES), BF)
    ahead = jnp.dot(earlier, stacked, preferred_element_type=F32).astype(BF)
    rank = jnp.dot(stacked, before, preferred_element_type=F32) + jnp.dot(ahead, ones, preferred_element_type=F32)
    place = jnp.full((chunks, LANES), -1.0, F32)
    for d in range(8):
        place = jnp.where(member[d] > 0, rank[d * chunks : (d + 1) * chunks] + d * per_peer, place)
    place = place.astype(jnp.int32)
    for j in range(chunks):
        place_ref[:, j * LANES : (j + 1) * LANES] = one_hot(place[j : j + 1], 8 * per_peer)

    half_way = groups // 2 * 4 * LANES

    def picked_by(first, last):
        x = rows_ref[:, :, first:last].reshape(FIELDS * LANES, last - first)
        return nt(x, place_ref[:, first:last])

    slot = slot_ref[...].astype(F32)
    for j in range(chunks // 4):
        part = slice(16 * j, 16 * j + 16)
        if j == groups // 2:
            picked = picked_by(0, half_way)
        slots = [jnp.broadcast_to(slot[4 * j + i : 4 * j + i + 1], (4, LANES)) for i in range(4)]
        extra = [ion_ref[part, :], jnp.concatenate(slots, axis=0).astype(BF)]
        extra = jnp.concatenate([e.reshape(1, 16, LANES) for e in extra], axis=0)
        copies[j].wait()
        for p in range(0, LANES, 16):
            x = held[j, p : min(p + 16, terms)]
            if p + 16 > terms:
                x = jnp.concatenate([x, extra, jnp.zeros((16 - x.shape[0] - 2, 16, LANES), BF)], axis=0)
            x = jnp.swapaxes(x, 0, 1)
            for i in range(4):
                lanes = slice((4 * j + i) * LANES, (4 * j + i + 1) * LANES)
                for f in range(FIELDS):
                    rows_ref[f, p : p + 16, lanes] = x[4 * i + f]

    picked = picked + picked_by(half_way, place_ref.shape[1])

    targets = {
        (1, 1): (x_even_ref, 0), (1, 0): (x_even_ref, 1), (1, 2): (x_even_ref, 2),
        (2, 1): (x_odd_ref, 0), (2, 0): (x_odd_ref, 1), (2, 2): (x_odd_ref, 2),
        (0, 1): (y_even_ref, 0), (0, 2): (y_odd_ref, 0),
    }
    lane = lax.broadcasted_iota(jnp.int32, (LANES, LANES), 1) // per_peer
    each = LANES // per_peer
    turned = []
    for half in range(2):
        x = [picked[f * LANES : (f + 1) * LANES, half * LANES : (half + 1) * LANES] for f in range(FIELDS)]
        turned.append([pltpu.roll(t, f * per_peer, 1) if f else t for f, t in enumerate(x)])
    for d, where in enumerate(AROUND):
        message = turned[d // each][0]
        for f in range(1, FIELDS):
            message = jnp.where(lane == (f + d) % each, turned[d // each][f], message)
        ref, at = targets[where]
        at = at * LANES + (SLAB_X if where[0] else 0)
        ref[at : at + LANES] = message.astype(BF)


def pack(sizes, owner, slot, table, multipoles, evaluation, ions):
    terms = multipoles.shape[0]
    atoms = slot.shape[0]
    chunks = atoms // LANES
    per_peer = atoms // 64
    whole = pl.BlockSpec(memory_space=pltpu.VMEM)
    view = evaluation.transpose(1, 0, 2).reshape(terms, FIELDS, chunks, LANES)
    view = view.transpose(0, 2, 1, 3).reshape(terms, FIELDS * chunks, LANES)
    ions = ions.reshape(FIELDS, chunks, LANES).transpose(1, 0, 2).reshape(FIELDS * chunks, LANES)
    block = lambda rows: jax.ShapeDtypeStruct((rows, LANES), BF)
    return pl.pallas_call(
        functools.partial(pack_kernel, sizes),
        in_specs=[pl.BlockSpec(memory_space=pl.ANY)] * 6,
        out_specs=[whole] * 7,
        out_shape=[block(LANES), block(SLAB_X + 3 * LANES), block(SLAB_X + 3 * LANES), block(LANES), block(LANES),
                   pltpu.VMEM((FIELDS, LANES, atoms), BF),
                   pltpu.VMEM((8 * per_peer, atoms), BF)],
        scratch_shapes=[
            pltpu.VMEM((chunks // 4, terms, 16, LANES), BF),
            pltpu.VMEM((chunks, LANES), jnp.int32),
            pltpu.VMEM((chunks, LANES), jnp.int32),
            pltpu.VMEM((8, LANES), jnp.int32),
            pltpu.VMEM((terms, LANES), BF),
            pltpu.VMEM((FIELDS * chunks, LANES), BF),
            pltpu.SemaphoreType.DMA((chunks // 4 + 5,)),
        ],
        compiler_params=pltpu.CompilerParams(vmem_limit_bytes=24 * 2**20),
        name="pack",
    )(*(pltpu.with_memory_space_constraint(x, pltpu.HBM) for x in (
        owner.reshape(chunks, LANES), slot.reshape(chunks, LANES), table, multipoles, view, ions)))


def tiles_of(ref, first, shape):
    nx, ny = shape
    value = ref[first : first + nx * ny * BZ, :].astype(F32)
    return {(x, y): value[(x * ny + y) * BZ : (x * ny + y + 1) * BZ] for x in range(nx) for y in range(ny)}


def forward_kernel(own, x_even, x_odd, y_even_message, y_odd_message, y_even_ref, y_odd_ref, odd_messages_ref):
    even_y = lax.rem(lax.axis_index("ys"), 2) == 0
    lower, upper = [], []
    for ref, nx in ((own, BX), (x_even, REACH), (x_odd, REACH)):
        tiles = tiles_of(ref, 0, (nx, BY))
        lower += [tiles[x, y] for x in range(nx) for y in range(REACH)]
        upper += [tiles[x, y + BY - REACH] for x in range(nx) for y in range(REACH)]
    lower, upper = jnp.concatenate(lower, axis=0), jnp.concatenate(upper, axis=0)
    y_even_ref[:SLAB_Y] = jnp.where(even_y, upper, lower).astype(BF)
    y_odd_ref[:SLAB_Y] = jnp.where(even_y, lower, upper).astype(BF)
    y_even_ref[SLAB_Y : SLAB_Y + LANES] = y_even_message[...]
    y_odd_ref[SLAB_Y:] = y_odd_message[...]
    for ref, to, at in ((y_even_ref, SLAB_Y + LANES, 0), (odd_messages_ref, 0, 2)):
        for i, source in enumerate((x_even, x_odd)):
            first = SLAB_X + at * LANES
            ref[to + i * LANES : to + (i + 1) * LANES] = source[first : first + LANES]


def forward(*operands):
    vmem = pl.BlockSpec(memory_space=pltpu.VMEM)
    return pl.pallas_call(
        forward_kernel,
        in_specs=[vmem] * 5,
        out_specs=[vmem] * 3,
        out_shape=[pltpu.VMEM((rows, LANES), BF) for rows in (SLAB_Y + 3 * LANES, SLAB_Y + LANES, 2 * LANES)],
        compiler_params=pltpu.CompilerParams(vmem_limit_bytes=4 * 2**20),
        name="forward",
    )(*operands)


def sources_along_x(own, x_even, x_odd):
    even_x = lax.rem(lax.axis_index("xs"), 2) == 0
    found = {(REACH + x, REACH + y): t for (x, y), t in tiles_of(own, 0, (BX, BY)).items()}
    a, b = tiles_of(x_even, 0, (REACH, BY)), tiles_of(x_odd, 0, (REACH, BY))
    for x, y in a:
        found[x, REACH + y] = jnp.where(even_x, b[x, y], a[x, y])
        found[REACH + BX + x, REACH + y] = jnp.where(even_x, a[x, y], b[x, y])
    return found


def sources_along_y(y_even, y_odd):
    even_x = lax.rem(lax.axis_index("xs"), 2) == 0
    even_y = lax.rem(lax.axis_index("ys"), 2) == 0
    strips = []
    for ref in (y_even, y_odd):
        strip = {(REACH + x, y): t for (x, y), t in tiles_of(ref, 0, (BX, REACH)).items()}
        first = BX * REACH * BZ
        a = tiles_of(ref, first, (REACH, REACH))
        b = tiles_of(ref, first + REACH * REACH * BZ, (REACH, REACH))
        for x, y in a:
            strip[x, y] = jnp.where(even_x, b[x, y], a[x, y])
            strip[REACH + BX + x, y] = jnp.where(even_x, a[x, y], b[x, y])
        strips.append(strip)
    found = {}
    for x, y in strips[0]:
        found[x, y] = jnp.where(even_y, strips[1][x, y], strips[0][x, y])
        found[x, REACH + BY + y] = jnp.where(even_y, strips[0][x, y], strips[1][x, y])
    return found


def inner_kernel(own, x_even, x_odd, shifted_ref, grid_ref):
    for (x, y), box in sources_along_x(own, x_even, x_odd).items():
        grid_ref[x, y] = box
    shift_sources(INNER, grid_ref, shifted_ref)


def inner_pairs(own, x_even, x_odd):
    vmem = pl.BlockSpec(memory_space=pltpu.VMEM)
    return pl.pallas_call(
        inner_kernel,
        in_specs=[vmem] * 3,
        out_specs=[vmem] * 2,
        out_shape=[pltpu.VMEM((NSHIFT * len(INNER) * EXT, 16, LANES), BF), pltpu.VMEM((EXT, REACH + BY, BZ, LANES), F32)],
        compiler_params=pltpu.CompilerParams(vmem_limit_bytes=8 * 2**20),
        cost_estimate=pl.CostEstimate(flops=0, bytes_accessed=3 * 2**20, transcendentals=0),
        name="inner_pairs",
    )(own, x_even, x_odd)


def messages(x_even, x_odd, y_even, y_odd, odd_passed):
    direct = SLAB_X + LANES
    return [
        (x_even, direct), (y_even, SLAB_Y + LANES), (odd_passed, 0),
        (x_odd, direct), (y_even, SLAB_Y + 2 * LANES), (odd_passed, LANES),
        (y_even, SLAB_Y), (y_odd, SLAB_Y),
    ]


def m2l_kernel(inner, along_x, y_odd, y_even, first_ref, second_ref, local_ref, grid, outer):
    for (x, y), box in sources_along_y(y_even, y_odd).items():
        grid[x, y] = box
    for x in range(EXT):
        for y in (REACH, REACH + BY - 1):
            grid[x, y] = along_x[x, y]
    shift_sources(OUTER, grid, outer)
    listed = offsets()
    acc = jnp.zeros((LANES, LANES), F32)
    for k0 in range(0, len(listed), STEP):
        some = range(k0, min(k0 + STEP, len(listed)))
        a = [jnp.concatenate([first_ref[k], second_ref[k]], axis=0) for k in some]
        b = [shifted_sources(inner, outer, listed[k]) for k in some]
        acc = acc + nt(jnp.concatenate(a, axis=1), jnp.concatenate(b, axis=1))
    local_ref[...] = acc.astype(BF)


def m2l(inner, along_x, y_odd, y_even, first, second):
    vmem = pl.BlockSpec(memory_space=pltpu.VMEM)
    pinned = [pltpu.with_memory_space_constraint(x, pltpu.VMEM) for x in (inner, along_x, first, second)]
    return pl.pallas_call(
        m2l_kernel,
        in_specs=[vmem] * 6,
        out_specs=vmem,
        out_shape=jax.ShapeDtypeStruct((LANES, LANES), BF),
        scratch_shapes=[
            pltpu.VMEM((EXT, EXT, BZ, LANES), F32),
            pltpu.VMEM((NSHIFT * len(OUTER) * EXT, 16, LANES), BF),
        ],
        compiler_params=pltpu.CompilerParams(vmem_limit_bytes=16 * 2**20),
        cost_estimate=pl.CostEstimate(flops=0, bytes_accessed=2**16, transcendentals=0),
        name="m2l",
    )(pinned[0], pinned[1], y_odd, y_even, pinned[2], pinned[3])


def answer_kernel(terms, local_ref, x_odd, x_even, y_odd, y_even, odd_passed, by_even_ref, by_odd_ref, by_y_ref, tail_ref):
    local = local_ref[...]
    row = lax.broadcasted_iota(jnp.int32, (8, LANES), 0)
    answers = []
    for i, (ref, at) in enumerate(messages(x_even, x_odd, y_even, y_odd, odd_passed)):
        x = ref[at : at + LANES, :].astype(F32)
        tail_ref[i : i + 1] = x[terms : terms + 1]
        tail_ref[8 + i : 9 + i] = x[terms + 1 : terms + 2]
        spread = one_hot(x[terms + 1 : terms + 2].astype(jnp.int32), LANES)
        column = jnp.dot(local, spread, preferred_element_type=F32)
        answers.append(jnp.sum(x[:terms] * column[:terms], axis=0, keepdims=True))
    for ref, first in ((by_even_ref, 0), (by_odd_ref, 3), (by_y_ref, 6)):
        tile = jnp.zeros((8, LANES), F32)
        for i in range(min(3, 8 - first)):
            tile = jnp.where(row == i, answers[first + i], tile)
        ref[...] = tile


def answer(terms, *operands):
    vmem = pl.BlockSpec(memory_space=pltpu.VMEM)
    return pl.pallas_call(
        functools.partial(answer_kernel, terms),
        in_specs=[vmem] * 6,
        out_specs=[vmem] * 4,
        out_shape=[jax.ShapeDtypeStruct((8, LANES), F32)] * 3 + [jax.ShapeDtypeStruct((16, LANES), F32)],
        compiler_params=pltpu.CompilerParams(vmem_limit_bytes=4 * 2**20),
        name="answer",
    )(*operands)


def atoms_kernel(size_y, owner_ref, slot_ref, ion_ref, rows_ref, local_ref, tail_ref,
                 by_even_ref, by_odd_ref, by_y_ref, local_exp_ref, far_ref, virial_ref):
    chunks = slot_ref.shape[0]
    local = local_ref[...]
    local_exp_ref[...] = local[: local_exp_ref.shape[0]]
    slots = jnp.where(owner_ref[...] == lax.axis_index("xs") * size_y + lax.axis_index("ys"), slot_ref[...], -1)
    row = lax.broadcasted_iota(jnp.int32, (8, LANES), 0)
    total = jnp.zeros((9 * 8, LANES), F32)
    for j in range(chunks):
        lanes = slice(j * LANES, (j + 1) * LANES)
        spread = one_hot(slots[j : j + 1], LANES)
        column = jnp.dot(local, spread, preferred_element_type=F32)
        far = jnp.zeros((8, LANES), F32)
        for f in range(FIELDS):
            value = jnp.sum(rows_ref[f, :, lanes].astype(F32) * column, axis=0, keepdims=True)
            far = jnp.where(row == f, value, far)
        far_ref[:, lanes] = far[:FIELDS]
        ion = ion_ref[j * FIELDS : (j + 1) * FIELDS, :].astype(F32)
        terms3 = jnp.concatenate([ion[0:1] * ion[a : a + 1] * far for a in (1, 2, 3)], axis=0)
        total = total + nt(split3(terms3), spread)

    per_peer = by_y_ref.shape[1] // FIELDS
    group = lax.broadcasted_iota(jnp.int32, (8, LANES), 1) // per_peer
    answers = [(ref, i) for ref in (by_even_ref, by_odd_ref) for i in range(3)] + [(by_y_ref, 0), (by_y_ref, 1)]
    for n, (answer, i) in enumerate(answers):
        d = AROUND.index(SENDERS[n])
        spread = one_hot(tail_ref[8 + n : 9 + n].astype(jnp.int32), LANES)
        ion = jnp.broadcast_to(tail_ref[n : n + 1], (8, LANES))

        def everywhere(f):
            x = jnp.where(group == (f + d) % FIELDS, ion, 0.0)
            x = x + pltpu.roll(x, 2 * per_peer, 1)
            return x + pltpu.roll(x, per_peer, 1)

        far = jnp.where(group == (row + d) % FIELDS, jnp.broadcast_to(answer[i : i + 1, :], (8, LANES)), 0.0)
        charge = everywhere(0)
        terms3 = jnp.concatenate([charge * everywhere(a) * far for a in (1, 2, 3)], axis=0)
        total = total + nt(split3(terms3), spread)
    virial = total[:24] + total[24:48] + total[48:]
    for a in range(3):
        virial_ref[3 * a : 3 * a + 3, :] = virial[8 * a + 1 : 8 * a + 4]


def atoms_of_device(terms, size_y, owner, slot, ions, rows, local, tail, down, up_, side):
    atoms = slot.shape[0]
    chunks = atoms // LANES
    whole = pl.BlockSpec(memory_space=pltpu.VMEM)
    ions = ions.reshape(FIELDS, chunks, LANES).transpose(1, 0, 2).reshape(FIELDS * chunks, LANES)
    return pl.pallas_call(
        functools.partial(atoms_kernel, size_y),
        in_specs=[whole] * 9,
        out_specs=[whole] * 3,
        out_shape=[jax.ShapeDtypeStruct((terms, LANES), BF), jax.ShapeDtypeStruct((FIELDS, atoms), F32),
                   jax.ShapeDtypeStruct((9, LANES), F32)],
        compiler_params=pltpu.CompilerParams(vmem_limit_bytes=16 * 2**20),
        cost_estimate=pl.CostEstimate(flops=4 * 10**6, bytes_accessed=8 * 2**20, transcendentals=0),
        name="atoms",
    )(owner.reshape(chunks, LANES), slot.reshape(chunks, LANES), ions, pltpu.with_memory_space_constraint(rows, pltpu.VMEM), local, tail, down, up_, side)


def turn_kernel(answer_y, x_even, x_odd, y_odd_ref, y_even_ref):
    for n, ref in ((1, y_even_ref), (2, y_odd_ref)):
        ref[...] = jnp.zeros(ref.shape, F32)
        ref[0:1] = answer_y[n - 1 : n]
        ref[1:2] = x_even[n : n + 1]
        ref[2:3] = x_odd[n : n + 1]


def turn(*operands):
    vmem = pl.BlockSpec(memory_space=pltpu.VMEM)
    return pl.pallas_call(
        turn_kernel,
        in_specs=[vmem] * 3,
        out_specs=[vmem] * 2,
        out_shape=[jax.ShapeDtypeStruct((8, LANES), F32)] * 2,
        compiler_params=pltpu.CompilerParams(vmem_limit_bytes=2**20),
        name="turn",
    )(*operands)


def merge_kernel(far_ref, place_ref, x_odd, x_even, y_odd, y_even, out_ref):
    per_peer = place_ref.shape[0] // 8
    each = LANES // per_peer
    returned = {
        (1, 0): (x_even, 0), (2, 0): (x_odd, 0),
        (0, 1): (y_even, 0), (1, 1): (y_even, 1), (2, 1): (y_even, 2),
        (0, 2): (y_odd, 0), (1, 2): (y_odd, 1), (2, 2): (y_odd, 2),
    }
    row = lax.broadcasted_iota(jnp.int32, (8, LANES), 0)
    group = lax.broadcasted_iota(jnp.int32, (8, LANES), 1) // per_peer
    halves = []
    for half in range(2):
        x = []
        for where in AROUND[half * each : half * each + each]:
            ref, i = returned[where]
            x.append(jnp.broadcast_to(ref[i : i + 1, :], (8, LANES)))
        tile = jnp.zeros((8, LANES), F32)
        for f in range(FIELDS):
            y = x[0]
            for g in range(1, each):
                y = jnp.where(group == (f + g) % each, x[g], y)
            tile = jnp.where(row == f, pltpu.roll(y, (each - f) * per_peer, 1) if f else y, tile)
        halves.append(tile)
    back = split3(jnp.concatenate(halves, axis=1))
    added = jnp.dot(back, place_ref[...], preferred_element_type=F32)
    out_ref[...] = far_ref[...] + (added[:FIELDS] + added[8 : 8 + FIELDS] + added[16 : 16 + FIELDS])


def merge(far, place, *returned):
    whole = pl.BlockSpec(memory_space=pltpu.VMEM)
    return pl.pallas_call(
        merge_kernel,
        in_specs=[whole] * 6,
        out_specs=whole,
        out_shape=jax.ShapeDtypeStruct(far.shape, F32),
        compiler_params=pltpu.CompilerParams(vmem_limit_bytes=16 * 2**20),
        name="merge",
    )(far, pltpu.with_memory_space_constraint(place, pltpu.VMEM), *returned)


def across(axis, edge, block):
    count = lax.axis_size(axis)
    pairs = [(i, (i + 1) % count) for i in range(edge - 1, count, 2)]
    return lax.ppermute(block, axis, pairs + [(b, a) for a, b in pairs])


def shards(
    multipoles,
    translation_ops,
    target_interaction_table,
    evaluation,
    ion_data,
    atom_owner,
    atom_slot,
):
    num_terms = multipoles.shape[0]
    size_x = lax.axis_size("xs")
    size_y = lax.axis_size("ys")
    own, to_x_even, to_x_odd, y_even_message, y_odd_message, rows, place = pack(
        (size_x, size_y), atom_owner, atom_slot, target_interaction_table, multipoles, evaluation, ion_data
    )
    x_even = across("xs", 1, to_x_even)
    x_odd = across("xs", 2, to_x_odd)
    first = by_operator(translation_ops, 0, 6)
    x_even, x_odd, first = lax.optimization_barrier((x_even, x_odd, first))
    to_y_even, to_y_odd, odd_messages = forward(own, x_even, x_odd, y_even_message, y_odd_message)
    y_odd = across("ys", 2, to_y_odd)
    y_even = across("ys", 1, to_y_even)
    odd_messages = across("ys", 2, odd_messages)
    second = by_operator(translation_ops, 6, 2)
    inner, along_x = inner_pairs(own, x_even, x_odd)
    local = m2l(inner, along_x, y_odd, y_even, first, second)
    answer_x_even, answer_x_odd, answer_y, tail = answer(
        num_terms, local, x_odd, x_even, y_odd, y_even, odd_messages
    )

    back_x_even = across("xs", 1, answer_x_even)
    back_x_odd = across("xs", 2, answer_x_odd)
    local_exp, far, box_virial = atoms_of_device(
        num_terms, size_y, atom_owner, atom_slot, ion_data, rows, local, tail, answer_x_even, answer_x_odd, answer_y
    )
    back_x_even, back_x_odd, far = lax.optimization_barrier((back_x_even, back_x_odd, far))
    answer_y_odd, answer_y_even = turn(answer_y, back_x_even, back_x_odd)
    back_y_odd = across("ys", 2, answer_y_odd)
    back_y_even = across("ys", 1, answer_y_even)
    atom_far_field = merge(far, place, back_x_odd, back_x_even, back_y_odd, back_y_even)
    return (local_exp, atom_far_field, box_virial)


def solution(mesh):
    placed = (
        P(None, ("xs", "ys")),
        P(),
        P(None, ("xs", "ys")),
        P(None, None, ("xs", "ys")),
        P(None, ("xs", "ys")),
        P(("xs", "ys"), None),
        P(("xs", "ys")),
    )
    return jax.shard_map(
        shards,
        mesh=mesh,
        in_specs=placed,
        out_specs=(P(None, ("xs", "ys")), P(None, ("xs", "ys")), P(None, ("xs", "ys"))),
        check_vma=False,
    )
```
